256 devices in a mesh: dp: 64 (over y, x, z_lo, core), tensor: 4 (over z_hi).
Axes of the slice: x: 4, y: 4, z: 8 (z_hi: 4, z_lo: 2; z = z_hi * 2 + z_lo), core: 2. Of those that a mesh axis runs over, the one named last changes fastest.
Arguments:
- base_codes: int32 [4096, 14336], P('dp', 'tensor'), may hold values from 0 to 15
- block_scales: float32 [4096, 224], P('dp', 'tensor'), may hold values from 0.0008 to 0.0176, as said below
- input_adapter_factor: bfloat16 [4096, 64], replicated, may hold values from -0.09375 to 0.09375
- output_adapter_factor: bfloat16 [64, 14336], P(None, 'tensor'), may hold values from -0.046875 to 0.046875
- magnitude: float32 [14336], P('tensor'), may hold values from 0.5 to 2
- inputs: bfloat16 [12288, 4096], P('dp', 'tensor'), may hold values from -6 to 6
- grad_out: bfloat16 [12288, 14336], P('dp', 'tensor'), may hold values from -1.5 to 1.5
- pre_scale: bfloat16 [12288, 14336], P('dp', 'tensor'), may hold values from -6 to 6
Outputs:
- grad_inputs: bfloat16 [12288, 4096], P('dp', 'tensor')
- input_adapter_gradient: float32 [4096, 64], P('tensor')
- output_adapter_gradient: float32 [64, 14336], P(None, 'tensor')
- grad_magnitude: float32 [14336], P('tensor')
The draws below stay inside these ranges and needn't reach their ends.
Inputs may be any that keep to these rules, and one draw needn't show every extreme that they name: `block_scales`: block scales of the 4-bit codes.
All inputs are finite; a program needn't handle non-finite values.
Results may differ from the reference program's by a relative error of at most 0.015.
Values may be sent and summed in bfloat16 or wider, within the bound.
No kernel may reach another device: no remote copies, remote signals or barrier semaphores. Data moves between devices by JAX's collectives and lax.ppermute only.
A program may use at most 192 MiB of HBM per device.

```python
import math
import jax
import jax.numpy as jnp
from jax import lax

D = 4096
FF = 14336
R = 64
QBLOCK = 64
TOKENS = 12288
N_TENSOR = 4


def draw_block_scales(key, part):
    key = jax.random.fold_in(key, 7)
    grid_shape = (D, FF // QBLOCK)
    position = jnp.arange(D, dtype=jnp.float32) / D
    values = jnp.exp(jax.random.uniform(key, grid_shape, jnp.float32, math.log(0.0008), math.log(0.008)))
    row_ramp = 1.0 + 0.75 * position
    return values * row_ramp[:, None]


def touch_ends(values, key, low, top_value):
    longest = values.shape.index(max(values.shape))
    spots = []
    for shift in (0, 1):
        where = [jax.random.randint(jax.random.fold_in(key, axis), (), 0, length) for axis, length in enumerate(values.shape)]
        where[longest] = (where[longest] + shift) % values.shape[longest]
        spots.append(tuple(where))
    return values.at[spots[0]].set(low).at[spots[1]].set(top_value)


def block_scale(stream_key, shape, split, smallest, top_value):
    level = 1.0
    for dim, shards_of in split:
        heights = jax.random.uniform(jax.random.fold_in(jax.random.fold_in(stream_key, 6), dim), (shards_of,), jnp.float32, smallest / len(split), top_value / len(split))
        level = level * jnp.repeat(jnp.exp(heights), shape[dim] // shards_of).reshape((-1,) + (1,) * (len(shape) - 1 - dim))
    return level


def noise(own_key, shape, deviation, limit, shards=(), kind=jnp.bfloat16):
    array = jax.random.normal(own_key, shape, jnp.float32) * deviation
    if len(shards) > 0:
        array = block_scale(own_key, shape, shards, -0.22, 0.18) * array
    return jnp.clip(array, min=-limit, max=limit).astype(kind)


def setup_inputs(seed: int = 0) -> dict:
    arg_keys = jax.random.split(jax.random.key(seed), 9)
    return {
        "base_codes": touch_ends(jax.random.randint(arg_keys[0], (D, FF), 0, 16), jax.random.fold_in(arg_keys[0], 1), 0, 15).astype(jnp.int32),
        "block_scales": draw_block_scales(jax.random.fold_in(arg_keys[8], 71), 0),
        "input_adapter_factor": noise(arg_keys[2], (D, R), D ** -0.5, 0.09375),
        "output_adapter_factor": noise(arg_keys[3], (R, FF), FF ** -0.5, 0.046875, ((1, 4),)),
        "magnitude": jnp.clip(jnp.exp(math.log(2.0) - 1.3862944 * jax.random.uniform(arg_keys[4], (FF,), jnp.float32) ** block_scale(arg_keys[4], (FF,), ((0, 4),), -0.2, 0.2)), 0.5, 2.0),
        "inputs": noise(arg_keys[5], (TOKENS, D), 1.0, 6.0, ((0, 64), (1, 4))),
        "grad_out": noise(arg_keys[6], (TOKENS, FF), 0.25, 1.5, ((0, 64), (1, 4))),
        "pre_scale": noise(arg_keys[7], (TOKENS, FF), 1.0, 6.0, ((0, 64), (1, 4))),
    }


adapter_scale_factor = 0.5

def dequantize(base_codes, block_scales, block_size):
    expanded = jnp.repeat(block_scales, block_size, axis=1)
    return (base_codes.astype(jnp.float32) - 7.5) * expanded

def reference(base_codes, block_scales, input_adapter_factor, output_adapter_factor, magnitude, inputs, grad_out, pre_scale):
    dequantized_weight = dequantize(base_codes, block_scales, QBLOCK)
    merged_weight_matrix = (dequantized_weight + adapter_scale_factor * jnp.dot(input_adapter_factor, output_adapter_factor, preferred_element_type=jnp.float32)).astype(jnp.bfloat16)
    merged_f = lax.optimization_barrier(merged_weight_matrix).astype(jnp.float32)
    col_norm = jnp.sqrt(lax.optimization_barrier(jnp.sum(merged_f * merged_f, axis=0)) + 1e-06)
    grad_f = grad_out.astype(jnp.float32)
    scaled_weight_matrix = (grad_f * (magnitude / col_norm)).astype(jnp.bfloat16)
    quarter = FF // N_TENSOR
    summed = jnp.zeros((inputs.shape[0], D), jnp.float32)
    for tensor_index in range(N_TENSOR):
        lower = tensor_index * quarter
        block_sum = jnp.dot(scaled_weight_matrix[:, lower:lower + quarter], merged_weight_matrix[:, lower:lower + quarter].T, preferred_element_type=jnp.float32)
        rounded = lax.optimization_barrier(block_sum.astype(jnp.bfloat16))
        summed = summed + rounded.astype(jnp.float32)
    grad_inputs = summed.astype(jnp.bfloat16)
    hidden_lowrank_term = jnp.dot(inputs, input_adapter_factor, preferred_element_type=jnp.float32).astype(jnp.bfloat16)
    backward_lowrank_term = jnp.dot(scaled_weight_matrix, output_adapter_factor.T, preferred_element_type=jnp.float32).astype(jnp.bfloat16)
    input_adapter_gradient = adapter_scale_factor * jnp.dot(inputs.T, backward_lowrank_term, preferred_element_type=jnp.float32)
    output_adapter_gradient = adapter_scale_factor * jnp.dot(hidden_lowrank_term.T, scaled_weight_matrix, preferred_element_type=jnp.float32)
    grad_magnitude = lax.optimization_barrier(jnp.sum(grad_f * pre_scale.astype(jnp.float32), axis=0)) / col_norm
    return (grad_inputs, input_adapter_gradient, output_adapter_gradient, grad_magnitude)
```

```python
import jax
import jax.numpy as jnp
from jax import lax
from jax.sharding import Mesh, PartitionSpec as P

SCALE = 0.5
BF = jnp.bfloat16
F32 = jnp.float32
SIZES = {"y": 4, "x": 4, "zl": 2, "co": 2, "t": 4}
DP = ("y", "x", "zl", "co")


def shift(value, axis, step):
    n = SIZES[axis]
    return lax.ppermute(value, axis, [(i, (i + step) % n) for i in range(n)])


def sum_over(value, axis):
    total = value
    for step in range(1, SIZES[axis]):
        total = total + shift(value, axis, step)
    return total


def place(buffer, block, row):
    return lax.dynamic_update_slice(buffer, block, (row, 0))


def on_device(codes, scales, in_factor, out_factor, magnitude, inputs, grad, pre):
    y, x, zl, co, t = (lax.axis_index(a) for a in ("y", "x", "zl", "co", "t"))
    rows, width = codes.shape
    tokens = grad.shape[0]
    half = tokens // 2
    features = inputs.shape[1]
    part = features // SIZES["x"]

    g_left = shift(grad, "x", 1)
    g_right = shift(grad, "x", -1)

    block = width // scales.shape[1]
    dequant = (codes.astype(F32) - 7.5) * jnp.repeat(scales, block, axis=1)
    first = (((y * 4 + x) * 2 + zl) * 2 + co) * rows
    factor_rows = lax.dynamic_slice_in_dim(in_factor, first, rows, 0)
    own = (
        dequant + SCALE * jnp.dot(factor_rows, out_factor, preferred_element_type=F32)
    ).astype(BF)

    other = shift(own, "zl", 1)
    squares = jnp.sum(jnp.square(own.astype(F32)), axis=0).reshape(-1, 128)
    weight = jnp.zeros((16 * rows, width), BF)

    def put(weight, block, step, zi):
        swapped = shift(block, "co", 1)
        row = ((y + step) % 4) * (4 * rows) + zi * (2 * rows)
        weight = place(weight, block, row + co * rows)
        return place(weight, swapped, row + (1 - co) * rows)

    for block_, zi in ((own, zl), (other, 1 - zl)):
        weight = put(weight, block_, 0, zi)
        down = shift(block_, "y", 1)
        up = shift(block_, "y", -1)
        weight = put(weight, down, -1, zi)
        weight = put(weight, up, 1, zi)
        h = rows // 2
        far = jnp.concatenate([shift(down[:h], "y", 1), shift(up[h:], "y", -1)], axis=0)
        weight = put(weight, far, 2, zi)

    for axis in ("co", "zl", "y", "x"):
        squares = sum_over(squares, axis)
    col_norm = jnp.sqrt(squares.reshape(-1) + 1e-06)
    ratio = magnitude / col_norm

    def scaled_of(g):
        return (g.astype(F32) * ratio).astype(BF)

    scaled_own = scaled_of(grad)

    factor_cols = lax.dynamic_slice_in_dim(in_factor, t * features, features, 0)
    hidden = jnp.dot(inputs, factor_cols, preferred_element_type=F32)
    back = lax.dot_general(
        scaled_own, out_factor, (((1,), (1,)), ((), ())), preferred_element_type=F32
    )
    low = jnp.concatenate([hidden, back], axis=1).astype(BF)
    low_sum = low.astype(F32)
    for step in (1, 2, 3):
        low_sum = low_sum + shift(low, "t", step).astype(F32)
    low_sum = low_sum.astype(BF)
    rank = hidden.shape[1]
    hidden, back = low_sum[:, :rank], low_sum[:, rank:]
    in_grad = SCALE * lax.dot_general(
        inputs, back, (((0,), (0,)), ((), ())), preferred_element_type=F32
    )
    out_grad = SCALE * lax.dot_general(
        hidden, scaled_own, (((0,), (0,)), ((), ())), preferred_element_type=F32
    )
    mag_grad = jnp.sum(grad.astype(F32) * pre.astype(F32), axis=0) / col_norm

    n = 64
    pieces = jnp.concatenate(
        [out_grad.reshape(n, -1), in_grad.reshape(n, -1), mag_grad.reshape(n, -1)], axis=1
    )
    got = lax.all_to_all(pieces, DP, 0, 0, tiled=True)
    mine = jnp.sum(got, axis=0)
    whole = lax.all_to_all(
        jnp.broadcast_to(mine[None], (n, mine.shape[0])), DP, 0, 0, tiled=True
    )
    a = out_grad.size // n
    b = a + in_grad.size // n
    out_grad = whole[:, :a].reshape(out_grad.shape)
    in_grad = whole[:, a:b].reshape(in_grad.shape)
    mag_grad = whole[:, b:].reshape(mag_grad.shape)

    g_far = jnp.concatenate(
        [shift(g_left[:half], "x", 1), shift(g_right[half:], "x", -1)], axis=0
    )

    def reduce_tile(gs):
        count = len(gs)
        scaled = jnp.concatenate([scaled_of(g) for g in gs], axis=0)
        tile = lax.dot_general(
            scaled, weight, (((1,), (1,)), ((), ())), preferred_element_type=F32
        ).astype(BF)
        m = tile.shape[0]
        c = [lax.dynamic_slice_in_dim(tile, ((t + e) % 4) * part, part, 1) for e in range(4)]
        k = m // 2
        to_right = shift(jnp.concatenate([c[2][:k], c[1][k:]], axis=0), "t", 1)
        to_left = shift(jnp.concatenate([c[3][:k], c[2][k:]], axis=0), "t", -1)
        fwd_right = (c[1][:k].astype(F32) + to_right[:k].astype(F32)).astype(BF)
        fwd_left = (c[3][k:].astype(F32) + to_left[k:].astype(F32)).astype(BF)
        got_top = shift(fwd_right, "t", 1)
        got_bottom = shift(fwd_left, "t", -1)
        top = c[0][:k].astype(F32) + got_top.astype(F32) + to_left[:k].astype(F32)
        bottom = c[0][k:].astype(F32) + to_right[k:].astype(F32) + got_bottom.astype(F32)
        total = jnp.concatenate([top, bottom], axis=0).astype(BF)
        return [total[i * tokens : (i + 1) * tokens] for i in range(count)]

    r_own, r_left, r_right = reduce_tile([grad, g_left, g_right])
    (r_far,) = reduce_tile([g_far])
    parts = [
        r_own,
        shift(r_left, "x", -1),
        shift(r_far, "x", 2),
        shift(r_right, "x", 1),
    ]
    grad_in = jnp.zeros((tokens, features), BF)
    for e, p in enumerate(parts):
        grad_in = lax.dynamic_update_slice(grad_in, p, (0, ((x + e) % 4) * part))
    return grad_in, in_grad, out_grad, mag_grad


def solution(mesh):
    fine = Mesh(mesh.devices.reshape(4, 4, 2, 2, 4), ("y", "x", "zl", "co", "t"))
    in_specs = (
        P(DP, "t"),
        P(DP, "t"),
        P(),
        P(None, "t"),
        P("t"),
        P(DP, "t"),
        P(DP, "t"),
        P(DP, "t"),
    )
    out_specs = (P(DP, "t"), P("t", None), P(None, "t"), P("t"))
    return jax.shard_map(
        on_device, mesh=fine, in_specs=in_specs, out_specs=out_specs, check_vma=False
    )
```

```python
import jax
import jax.numpy as jnp
from jax import lax
from jax.experimental import pallas as pl
from jax.experimental.pallas import tpu as pltpu
from jax.sharding import Mesh, PartitionSpec as P

SCALE = 0.5
BF = jnp.bfloat16
F32 = jnp.float32
SIZES = {"y": 4, "x": 4, "zl": 2, "co": 2, "t": 4}
DP = ("y", "x", "zl", "co")
N_DP = 64


def shift(value, axis, step):
    n = SIZES[axis]
    return lax.ppermute(value, axis, [(i, (i + step) % n) for i in range(n)])


def swap_all(value, axes):
    return lax.all_to_all(value, axes, 0, 0, tiled=True)


def merge_kernel(block, codes, scales, factor, out_factor, grad, pre, own, sums):
    width = codes.shape[1]
    count = scales.shape[1]
    start = pl.program_id(0) * width
    group = (start + lax.broadcasted_iota(jnp.int32, (count, width), 1)) // block
    pick = (group == lax.broadcasted_iota(jnp.int32, (count, width), 0)).astype(F32)
    spread = jnp.dot(
        scales[...], pick, precision=lax.Precision.HIGHEST, preferred_element_type=F32
    )
    low = jnp.dot(factor[...], out_factor[...], preferred_element_type=F32)
    merged = ((codes[...].astype(F32) - 7.5) * spread + SCALE * low).astype(BF)
    own[...] = merged
    wide = merged.astype(F32)
    sums[0:1, :] = jnp.sum(wide * wide, axis=0, keepdims=True)
    product = grad[...].astype(F32) * pre[...].astype(F32)
    sums[1:2, :] = jnp.sum(product, axis=0, keepdims=True)


def merge(codes, scales, factor, out_factor, grad, pre):
    rows, width = codes.shape
    tokens = grad.shape[0]
    rank = factor.shape[1]
    count = scales.shape[1]
    steps = 4
    part = width // steps

    def columns(n):
        return pl.BlockSpec((n, part), lambda i: (0, i))

    def whole(a, b):
        return pl.BlockSpec((a, b), lambda i: (0, 0))

    def body(*refs):
        merge_kernel(width // count, *refs)

    return pl.pallas_call(
        body,
        grid=(steps,),
        in_specs=[
            columns(rows),
            whole(rows, count),
            whole(rows, rank),
            columns(rank),
            columns(tokens),
            columns(tokens),
        ],
        out_specs=[columns(rows), columns(2)],
        out_shape=[
            jax.ShapeDtypeStruct((rows, width), BF),
            jax.ShapeDtypeStruct((2, width), F32),
        ],
        compiler_params=pltpu.CompilerParams(vmem_limit_bytes=32 * 1024 * 1024),
    )(codes, scales, factor, out_factor, grad, pre)


def on_device(codes, scales, in_factor, out_factor, magnitude, inputs, grad, pre):
    y, x, zl, co, t = (lax.axis_index(a) for a in ("y", "x", "zl", "co", "t"))
    rows, width = codes.shape
    tokens = grad.shape[0]
    half = tokens // 2
    features = inputs.shape[1]
    part = features // SIZES["x"]
    rank = in_factor.shape[1]

    g_left = shift(grad, "x", 1)
    g_right = shift(grad, "x", -1)

    first = (((y * 4 + x) * 2 + zl) * 2 + co) * rows
    factor_rows = lax.dynamic_slice_in_dim(in_factor, first, rows, 0)
    own, sums = merge(codes, scales, factor_rows, out_factor, grad, pre)
    other = shift(own, "zl", 1)

    sums = swap_all(sums.reshape(2, N_DP, -1).transpose(1, 0, 2).reshape(N_DP, -1), DP)
    sums = jnp.sum(sums, axis=0, keepdims=True)
    sums = swap_all(jnp.broadcast_to(sums, (N_DP, sums.shape[1])), DP)
    sums = sums.reshape(N_DP, 2, -1).transpose(1, 0, 2).reshape(2, width)
    col_norm = jnp.sqrt(sums[0] + 1e-06)
    mag_grad = sums[1] / col_norm
    ratio = magnitude / col_norm

    weight = jnp.zeros((4, 2, 2, rows, width), BF)

    def put(weight, block, step, zi):
        block = block.reshape(-1, rows, width)
        swapped = shift(block, "co", 1)
        row = (y + step) % 4
        for b, c in ((block, co), (swapped, 1 - co)):
            weight = lax.dynamic_update_slice(weight, b[None, :, None], (row, zi, c, 0, 0))
        return weight

    pair = jnp.where(zl == 0, jnp.stack([own, other]), jnp.stack([other, own]))
    down = shift(pair, "y", 1)
    up = shift(pair, "y", -1)
    weight = put(weight, pair, 0, 0)
    weight = put(weight, down, -1, 0)
    weight = put(weight, up, 1, 0)
    weight = put(weight, shift(down[0], "y", 1), 2, 0)
    weight = put(weight, shift(up[1], "y", -1), 2, 1)

    g_far = jnp.concatenate(
        [shift(g_left[:half], "x", 1), shift(g_right[half:], "x", -1)], axis=0
    )

    def scaled_of(g):
        return (g.astype(F32) * ratio).astype(BF)

    scaled_own = scaled_of(grad)
    scaled = jnp.zeros((4, tokens, width), BF)
    for e, g in ((0, scaled_own), (-1, scaled_of(g_left)), (1, scaled_of(g_right)), (2, scaled_of(g_far))):
        scaled = lax.dynamic_update_slice(scaled, g[None], ((x + e) % 4, 0, 0))

    factor_cols = lax.dynamic_slice_in_dim(in_factor, t * features, features, 0)
    hidden = jnp.dot(inputs, factor_cols, preferred_element_type=F32)
    back = lax.dot_general(
        scaled_own, out_factor, (((1,), (1,)), ((), ())), preferred_element_type=F32
    )
    low = jnp.concatenate([hidden, back], axis=1).astype(BF)
    low = swap_all(jnp.broadcast_to(low[None], (4,) + low.shape), "t")
    low = jnp.sum(low.astype(F32), axis=0).astype(BF)
    hidden, back = low[:, :rank], low[:, rank:]
    in_grad = SCALE * lax.dot_general(
        back, inputs, (((0,), (0,)), ((), ())), preferred_element_type=F32
    )
    out_grad = SCALE * lax.dot_general(
        hidden, scaled_own, (((0,), (0,)), ((), ())), preferred_element_type=F32
    )
    adapters = swap_all(jnp.concatenate([out_grad, in_grad], axis=1), DP)
    adapters = jnp.sum(adapters, axis=0, keepdims=True)
    adapters = swap_all(jnp.broadcast_to(adapters, (N_DP, adapters.shape[1])), DP)
    out_grad = adapters[:, :width]
    in_grad = adapters[:, width:].T

    tile = lax.dot_general(
        scaled.reshape(4 * tokens, width),
        weight.reshape(16 * rows, width),
        (((1,), (1,)), ((), ())),
        preferred_element_type=F32,
    ).astype(BF)
    tile = tile.reshape(4, tokens, 4, part).transpose(0, 2, 1, 3)
    tile = swap_all(tile.reshape(16, tokens, part), ("x", "t"))
    tile = jnp.sum(tile.reshape(4, 4, tokens, part).astype(F32), axis=1).astype(BF)
    grad_in = tile.transpose(1, 0, 2).reshape(tokens, features)
    return grad_in, in_grad, out_grad, mag_grad


def solution(mesh):
    fine = Mesh(mesh.devices.reshape(4, 4, 2, 2, 4), ("y", "x", "zl", "co", "t"))
    in_specs = (
        P(DP, "t"),
        P(DP, "t"),
        P(),
        P(None, "t"),
        P("t"),
        P(DP, "t"),
        P(DP, "t"),
        P(DP, "t"),
    )
    out_specs = (P(DP, "t"), P("t", None), P(None, "t"), P("t"))
    return jax.shard_map(
        on_device, mesh=fine, in_specs=in_specs, out_specs=out_specs, check_vma=False
    )
```

```python
import jax
import jax.numpy as jnp
from jax import lax
from jax.experimental import pallas as pl
from jax.experimental.pallas import tpu as pltpu
from jax.sharding import Mesh, PartitionSpec as P

SCALE = 0.5
BF = jnp.bfloat16
F32 = jnp.float32
SIZES = {"y": 4, "x": 4, "zl": 2, "co": 2, "t": 4}
DP = ("y", "x", "zl", "co")
N_DP = 64


def shift(value, axis, step):
    n = SIZES[axis]
    return lax.ppermute(value, axis, [(i, (i + step) % n) for i in range(n)])


def swap_all(value, axes):
    return lax.all_to_all(value, axes, 0, 0, tiled=True)


def after(value, *earlier):
    return lax.optimization_barrier((value,) + earlier)[0]


def merge_kernel(block, codes, scales, factor, out_factor, own, squares):
    width = codes.shape[1]
    count = scales.shape[1]
    start = pl.program_id(0) * width
    group = (start + lax.broadcasted_iota(jnp.int32, (count, width), 1)) // block
    pick = (group == lax.broadcasted_iota(jnp.int32, (count, width), 0)).astype(F32)
    spread = jnp.dot(
        scales[...], pick, precision=lax.Precision.HIGHEST, preferred_element_type=F32
    )
    low = jnp.dot(factor[...], out_factor[...], preferred_element_type=F32)
    merged = ((codes[...].astype(F32) - 7.5) * spread + SCALE * low).astype(BF)
    own[...] = merged
    wide = merged.astype(F32)
    squares[...] = jnp.sum(wide * wide, axis=0, keepdims=True)


def merge(codes, scales, factor, out_factor):
    rows, width = codes.shape
    rank = factor.shape[1]
    count = scales.shape[1]
    steps = 4
    part = width // steps

    def columns(n):
        return pl.BlockSpec((n, part), lambda i: (0, i))

    def whole(a, b):
        return pl.BlockSpec((a, b), lambda i: (0, 0))

    def body(*refs):
        merge_kernel(width // count, *refs)

    return pl.pallas_call(
        body,
        grid=(steps,),
        in_specs=[columns(rows), whole(rows, count), whole(rows, rank), columns(rank)],
        out_specs=[columns(rows), columns(1)],
        out_shape=[
            jax.ShapeDtypeStruct((rows, width), BF),
            jax.ShapeDtypeStruct((1, width), F32),
        ],
        compiler_params=pltpu.CompilerParams(vmem_limit_bytes=48 * 1024 * 1024),
    )(codes, scales, factor, out_factor)


def tile_kernel(where, grad, ratio, mine, swapped, out, scaled, wide):
    tokens = grad.shape[0]
    rows = mine.shape[2]
    co = where[0]

    @pl.when(pl.program_id(0) == 0)
    def _():
        @pl.loop(0, tokens, step=16)
        def _(r):
            r = pl.multiple_of(r, 16)
            value = grad[pl.ds(r, 16), :].astype(F32) * ratio[...]
            scaled[pl.ds(r, 16), :] = value.astype(BF)

    for zi in range(2):
        for source, c in ((mine, co), (swapped, 1 - co)):
            row = pl.multiple_of(zi * 2 * rows + c * rows, rows)
            wide[pl.ds(row, rows), :] = source[0, zi]
    n = tokens // 4
    for k in range(4):
        tile = lax.dot_general(
            scaled[k * n : (k + 1) * n, :],
            wide[...],
            (((1,), (1,)), ((), ())),
            preferred_element_type=F32,
        )
        out[k, 0] = tile.astype(BF)


def tile_of(where, grad, ratio, mine, swapped):
    tokens, width = grad.shape
    rows = mine.shape[2]
    n = tokens // 4

    def whole(shape):
        return pl.BlockSpec(shape, lambda i, w: (0, 0))

    weights = pl.BlockSpec((1, 2, rows, width), lambda i, w: (i, 0, 0, 0))
    return pl.pallas_call(
        tile_kernel,
        grid_spec=pltpu.PrefetchScalarGridSpec(
            num_scalar_prefetch=1,
            grid=(4,),
            in_specs=[whole(grad.shape), whole((1, width)), weights, weights],
            out_specs=pl.BlockSpec((4, 1, n, 4 * rows), lambda i, w: (0, i, 0, 0)),
            scratch_shapes=[
                pltpu.VMEM((tokens, width), BF),
                pltpu.VMEM((4 * rows, width), BF),
            ],
        ),
        out_shape=jax.ShapeDtypeStruct((4, 4, n, 4 * rows), BF),
        compiler_params=pltpu.CompilerParams(vmem_limit_bytes=48 * 1024 * 1024),
        cost_estimate=pl.CostEstimate(
            flops=2 * tokens * 16 * rows * width,
            bytes_accessed=2 * width * (tokens + 16 * rows),
            transcendentals=0,
        ),
    )(where, grad, ratio, mine, swapped)


def on_device(codes, scales, in_factor, out_factor, magnitude, inputs, grad, pre):
    y, x, zl, co, t = (lax.axis_index(a) for a in ("y", "x", "zl", "co", "t"))
    rows, width = codes.shape
    tokens = grad.shape[0]
    features = inputs.shape[1]
    part = features // SIZES["x"]
    rank = in_factor.shape[1]

    g_all = lax.all_gather(grad, "x", axis=0, tiled=True)

    first = (((y * 4 + x) * 2 + zl) * 2 + co) * rows
    factor_rows = lax.dynamic_slice_in_dim(in_factor, first, rows, 0)
    own, squares = merge(codes, scales, factor_rows, out_factor)

    other = shift(own, "zl", 1)
    mine = jnp.zeros((4, 2, rows, width), BF)

    def put(buffer, block, step, zi):
        return lax.dynamic_update_slice(buffer, block[None, None], ((y + step) % 4, zi, 0, 0))

    own_down, own_up = shift(own, "y", 1), shift(own, "y", -1)
    own_far = shift(own_down, "y", 1)
    other_down, other_up = shift(other, "y", 1), shift(other, "y", -1)
    other_far = shift(other_up, "y", -1)
    for zi, blocks in (
        (zl, ((own, 0), (own_down, -1), (own_up, 1), (own_far, 2))),
        (1 - zl, ((other, 0), (other_down, -1), (other_up, 1), (other_far, 2))),
    ):
        for block, step in blocks:
            mine = put(mine, block, step, zi)
    swapped = shift(mine, "co", 1)

    total = squares.reshape(-1, 128)
    for axis in ("y", "co", "zl", "x"):
        if axis == "x":
            total = after(total, own_down, own_up, other)
        steps = [shift(total, axis, k) for k in range(1, SIZES[axis])]
        for piece in steps:
            total = total + piece
    col_norm = jnp.sqrt(total.reshape(-1) + 1e-06)
    ratio = magnitude / col_norm

    scaled_own = (grad.astype(F32) * ratio).astype(BF)
    factor_cols = lax.dynamic_slice_in_dim(in_factor, t * features, features, 0)
    hidden = jnp.dot(inputs, factor_cols, preferred_element_type=F32)
    back = lax.dot_general(
        scaled_own, out_factor, (((1,), (1,)), ((), ())), preferred_element_type=F32
    )
    low = jnp.concatenate([hidden, back], axis=1).astype(BF)
    pieces = [shift(low, "t", k) for k in (1, 2, 3)]
    low = sum((p.astype(F32) for p in pieces), low.astype(F32)).astype(BF)
    hidden, back = low[:, :rank], low[:, rank:]
    in_grad = SCALE * lax.dot_general(
        back, inputs, (((0,), (0,)), ((), ())), preferred_element_type=F32
    )
    out_grad = SCALE * lax.dot_general(
        hidden, scaled_own, (((0,), (0,)), ((), ())), preferred_element_type=F32
    )
    mag_sum = jnp.sum(grad.astype(F32) * pre.astype(F32), axis=0).reshape(N_DP, -1)
    adapters = jnp.concatenate([out_grad, in_grad, mag_sum], axis=1)
    for axis, index in (("co", co), ("zl", zl)):
        side = adapters.shape[0] // 2
        keep = lax.dynamic_slice_in_dim(adapters, index * side, side, 0)
        give = lax.dynamic_slice_in_dim(adapters, (1 - index) * side, side, 0)
        adapters = keep + shift(give, axis, 1)
    adapters = swap_all(adapters, ("y", "x"))
    adapters = jnp.sum(adapters, axis=0, keepdims=True)
    adapters = swap_all(jnp.broadcast_to(adapters, (side, adapters.shape[1])), ("y", "x"))
    for axis, index in (("zl", zl), ("co", co)):
        across = shift(adapters, axis, 1)
        pair = (jnp.stack([adapters, across]), jnp.stack([across, adapters]))
        adapters = jnp.where(index == 0, *pair).reshape(-1, adapters.shape[1])
    out_grad = adapters[:, :width]
    in_grad = adapters[:, width : width + features].T
    mag_grad = adapters[:, width + features :].reshape(-1) / col_norm

    where = co.astype(jnp.int32).reshape(1)
    tile = tile_of(where, g_all, ratio.reshape(1, -1), mine, swapped)
    tile = swap_all(tile.reshape(16, tokens, part), ("x", "t"))

    tile = jnp.sum(tile.reshape(4, 4, tokens, part).astype(F32), axis=1).astype(BF)
    grad_in = tile.transpose(1, 0, 2).reshape(tokens, features)
    return grad_in, in_grad, out_grad, mag_grad


def solution(mesh):
    fine = Mesh(mesh.devices.reshape(4, 4, 2, 2, 4), ("y", "x", "zl", "co", "t"))
    in_specs = (
        P(DP, "t"),
        P(DP, "t"),
        P(),
        P(None, "t"),
        P("t"),
        P(DP, "t"),
        P(DP, "t"),
        P(DP, "t"),
    )
    out_specs = (P(DP, "t"), P("t", None), P(None, "t"), P("t"))
    return jax.shard_map(
        on_device, mesh=fine, in_specs=in_specs, out_specs=out_specs, check_vma=False
    )
```

```python
import jax
import jax.numpy as jnp
from jax import lax
from jax.experimental import pallas as pl
from jax.experimental.pallas import tpu as pltpu
from jax.sharding import Mesh, PartitionSpec as P

SCALE = 0.5
BF = jnp.bfloat16
F32 = jnp.float32
SIZES = {"y": 4, "x": 4, "zl": 2, "co": 2, "t": 4}
DP = ("y", "x", "zl", "co")
N_DP = 64


def shift(value, axis, step):
    n = SIZES[axis]
    return lax.ppermute(value, axis, [(i, (i + step) % n) for i in range(n)])


def swap_all(value, axes):
    return lax.all_to_all(value, axes, 0, 0, tiled=True)


def after(value, *earlier):
    return lax.optimization_barrier((value,) + earlier)[0]


def merge_kernel(block, codes, scales, factor, out_factor, own, squares):
    width = codes.shape[1]
    count = scales.shape[0]
    start = pl.program_id(0) * width
    group = (start + lax.broadcasted_iota(jnp.int32, (count, width), 1)) // block
    pick = (group == lax.broadcasted_iota(jnp.int32, (count, width), 0)).astype(F32)
    spread = lax.dot_general(
        scales[...],
        pick,
        (((0,), (0,)), ((), ())),
        precision=lax.Precision.HIGHEST,
        preferred_element_type=F32,
    )
    low = jnp.dot(factor[...], out_factor[...], preferred_element_type=F32)
    merged = ((codes[...].astype(F32) - 7.5) * spread + SCALE * low).astype(BF)
    own[...] = merged
    wide = merged.astype(F32)
    squares[...] = jnp.sum(wide * wide, axis=0, keepdims=True)


def merge(codes, scales, factor, out_factor):
    rows, width = codes.shape
    rank = factor.shape[1]
    count = scales.shape[0]
    steps = 4
    part = width // steps

    def columns(n):
        return pl.BlockSpec((n, part), lambda i: (0, i))

    def whole(a, b):
        return pl.BlockSpec((a, b), lambda i: (0, 0))

    def body(*refs):
        merge_kernel(width // count, *refs)

    return pl.pallas_call(
        body,
        grid=(steps,),
        in_specs=[columns(rows), whole(count, rows), whole(rows, rank), columns(rank)],
        out_specs=[columns(rows), columns(1)],
        out_shape=[
            jax.ShapeDtypeStruct((rows, width), BF),
            jax.ShapeDtypeStruct((1, width), F32),
        ],
        compiler_params=pltpu.CompilerParams(vmem_limit_bytes=60 * 1024 * 1024),
    )(codes, scales, factor, out_factor)


def tile_kernel(where, scaled, own, other, own_swap, other_swap, out, wide):
    rows = own.shape[1]
    x, zl, co = where[0], where[1], where[2]
    for source, zi, c in (
        (own, zl, co),
        (other, 1 - zl, co),
        (own_swap, zl, 1 - co),
        (other_swap, 1 - zl, 1 - co),
    ):
        row = pl.multiple_of((zi * 2 + c) * rows, rows)
        wide[pl.ds(row, rows), :] = source[0]
    tile = lax.dot_general(
        scaled[...], wide[...], (((1,), (1,)), ((), ())), preferred_element_type=F32
    ).astype(BF)
    n = scaled.shape[0] // 4
    for k, e in enumerate((0, 3, 1, 2)):
        out[lax.rem(x + e, 4), 0] = tile[k * n : (k + 1) * n, :]


def tile_of(where, scaled, weights):
    tokens, width = scaled.shape
    rows = weights[0].shape[1]
    n = tokens // 4
    weight = pl.BlockSpec((1, rows, width), lambda i, w: (i, 0, 0))
    return pl.pallas_call(
        tile_kernel,
        grid_spec=pltpu.PrefetchScalarGridSpec(
            num_scalar_prefetch=1,
            grid=(4,),
            in_specs=[pl.BlockSpec((tokens, width), lambda i, w: (0, 0))] + [weight] * 4,
            out_specs=pl.BlockSpec((4, 1, n, 4 * rows), lambda i, w: (0, i, 0, 0)),
            scratch_shapes=[pltpu.VMEM((4 * rows, width), BF)],
        ),
        out_shape=jax.ShapeDtypeStruct((4, 4, n, 4 * rows), BF),
        compiler_params=pltpu.CompilerParams(vmem_limit_bytes=40 * 1024 * 1024),
        cost_estimate=pl.CostEstimate(
            flops=2 * tokens * 16 * rows * width,
            bytes_accessed=2 * width * (tokens + 16 * rows),
            transcendentals=0,
        ),
    )(where, scaled, *weights)


def on_device(codes, scales, in_factor, out_factor, magnitude, inputs, grad, pre):
    y, x, zl, co, t = (lax.axis_index(a) for a in ("y", "x", "zl", "co", "t"))
    rows, width = codes.shape
    tokens = grad.shape[0]
    half = tokens // 2
    features = inputs.shape[1]
    part = features // SIZES["x"]
    rank = in_factor.shape[1]

    low_half, high_half = grad[:half], grad[half:]
    left_low, right_high = shift(low_half, "x", 1), shift(high_half, "x", -1)
    left_high, right_low = shift(high_half, "x", 1), shift(low_half, "x", -1)
    far_low, far_high = shift(left_low, "x", 1), shift(right_high, "x", -1)

    first = (((y * 4 + x) * 2 + zl) * 2 + co) * rows
    factor_rows = lax.dynamic_slice_in_dim(in_factor, first, rows, 0)
    own, squares = merge(codes, scales.T, factor_rows, out_factor)

    other = shift(own, "zl", 1)
    own_down, own_up = shift(own, "y", 1), shift(own, "y", -1)
    own_far = shift(own_down, "y", 1)
    other_down, other_up = shift(other, "y", 1), shift(other, "y", -1)
    other_far = shift(other_up, "y", -1)

    def in_order(blocks):
        buffer = jnp.zeros((4, rows, width), BF)
        for block, step in zip(blocks, (0, -1, 1, 2)):
            buffer = lax.dynamic_update_slice(buffer, block[None], ((y + step) % 4, 0, 0))
        return buffer

    own_rows = in_order((own, own_down, own_up, own_far))
    own_swap = shift(own_rows, "co", 1)
    other_rows = in_order((other, other_down, other_up, other_far))
    other_swap = shift(other_rows, "co", 1)

    total = squares.reshape(-1, 128)
    for axis in ("y", "co", "zl", "x"):
        if axis == "x":
            total = after(total, own_down, own_up, left_low, right_high)
        steps = [shift(total, axis, k) for k in range(1, SIZES[axis])]
        for piece in steps:
            total = total + piece
    total = after(total, left_high, right_low)
    col_norm = jnp.sqrt(total.reshape(-1) + 1e-06)
    ratio = magnitude / col_norm

    def scaled_of(g):
        return (g.astype(F32) * ratio).astype(BF)

    scaled_own = scaled_of(grad)
    scaled = jnp.zeros((4 * tokens, width), BF)
    pieces = (grad, left_low, left_high, right_low, right_high, far_low, far_high)
    for k, g in zip((0, 2, 3, 4, 5, 6, 7), pieces):
        scaled = lax.dynamic_update_slice(scaled, scaled_of(g), (k * half, 0))

    factor_cols = lax.dynamic_slice_in_dim(in_factor, t * features, features, 0)
    hidden = jnp.dot(inputs, factor_cols, preferred_element_type=F32)
    back = lax.dot_general(
        scaled_own, out_factor, (((1,), (1,)), ((), ())), preferred_element_type=F32
    )
    low = jnp.concatenate([hidden, back], axis=1).astype(BF)
    low = after(low, own_far, other_down, other_up)
    pieces = [shift(low, "t", k) for k in (1, 2, 3)]
    low = sum((p.astype(F32) for p in pieces), low.astype(F32)).astype(BF)
    hidden, back = low[:, :rank], low[:, rank:]
    in_grad = SCALE * lax.dot_general(
        back, inputs, (((0,), (0,)), ((), ())), preferred_element_type=F32
    )
    out_grad = SCALE * lax.dot_general(
        hidden, scaled_own, (((0,), (0,)), ((), ())), preferred_element_type=F32
    )
    mag_sum = jnp.sum(grad.astype(F32) * pre.astype(F32), axis=0).reshape(N_DP, -1)
    adapters = jnp.concatenate([out_grad, in_grad, mag_sum], axis=1)
    adapters = after(adapters, other_far)
    side = adapters.shape[0] // 2
    keep = lax.dynamic_slice_in_dim(adapters, co * side, side, 0)
    give = lax.dynamic_slice_in_dim(adapters, (1 - co) * side, side, 0)
    adapters = keep + shift(give, "co", 1)
    adapters = adapters + shift(adapters, "zl", 1)
    adapters = after(adapters, far_low, far_high)
    for axis, index in (("y", y), ("x", x)):
        side = adapters.shape[0] // 4
        total = lax.dynamic_slice_in_dim(adapters, index * side, side, 0)
        for k in (1, 2, 3):
            give = lax.dynamic_slice_in_dim(adapters, ((index + k) % 4) * side, side, 0)
            total = total + shift(give, axis, k)
        adapters = total
    where = jnp.stack([x, zl, co]).astype(jnp.int32)
    tile = tile_of(where, scaled, (own_rows, other_rows, own_swap, other_swap))
    adapters = after(adapters, tile)
    tile = swap_all(tile.reshape(16, tokens, part), ("x", "t"))

    for axis, index in (("x", x), ("y", y), ("co", co)):
        n = SIZES[axis]
        side = adapters.shape[0]
        total = jnp.zeros((n * side, adapters.shape[1]), F32)
        for k in range(n):
            got = shift(adapters, axis, k) if k else adapters
            total = lax.dynamic_update_slice(total, got, (((index - k) % n) * side, 0))
        adapters = total
    out_grad = adapters[:, :width]
    in_grad = adapters[:, width : width + features].T
    mag_grad = adapters[:, width + features :].reshape(-1) / col_norm

    tile = jnp.sum(tile.reshape(4, 4, tokens, part).astype(F32), axis=1).astype(BF)
    grad_in = tile.transpose(1, 0, 2).reshape(tokens, features)
    return grad_in, in_grad, out_grad, mag_grad


def solution(mesh):
    fine = Mesh(mesh.devices.reshape(4, 4, 2, 2, 4), ("y", "x", "zl", "co", "t"))
    in_specs = (
        P(DP, "t"),
        P(DP, "t"),
        P(),
        P(None, "t"),
        P("t"),
        P(DP, "t"),
        P(DP, "t"),
        P(DP, "t"),
    )
    out_specs = (P(DP, "t"), P("t", None), P(None, "t"), P("t"))
    return jax.shard_map(
        on_device, mesh=fine, in_specs=in_specs, out_specs=out_specs, check_vma=False
    )
```

```python
import jax
import jax.numpy as jnp
from jax import lax
from jax.experimental import pallas as pl
from jax.experimental.pallas import tpu as pltpu
from jax.sharding import Mesh, PartitionSpec as P

SCALE = 0.5
BF = jnp.bfloat16
F32 = jnp.float32
SIZES = {"y": 4, "x": 4, "zl": 2, "co": 2, "t": 4}
DP = ("y", "x", "zl", "co")
N_DP = 64


def shift(value, axis, step):
    n = SIZES[axis]
    return lax.ppermute(value, axis, [(i, (i + step) % n) for i in range(n)])


def swap_all(value, axes):
    return lax.all_to_all(value, axes, 0, 0, tiled=True)


def after(value, *earlier):
    return lax.optimization_barrier((value,) + earlier)[0]


def merge_kernel(block, codes, scales, factor, out_factor, own, squares):
    width = codes.shape[1]
    count = scales.shape[0]
    start = pl.program_id(0) * width
    group = (start + lax.broadcasted_iota(jnp.int32, (count, width), 1)) // block
    pick = (group == lax.broadcasted_iota(jnp.int32, (count, width), 0)).astype(F32)
    spread = lax.dot_general(
        scales[...],
        pick,
        (((0,), (0,)), ((), ())),
        precision=lax.Precision.HIGHEST,
        preferred_element_type=F32,
    )
    low = jnp.dot(factor[...], out_factor[...], preferred_element_type=F32)
    merged = ((codes[...].astype(F32) - 7.5) * spread + SCALE * low).astype(BF)
    own[...] = merged
    wide = merged.astype(F32)
    squares[...] = jnp.sum(wide * wide, axis=0, keepdims=True)


def merge(codes, scales, factor, out_factor):
    rows, width = codes.shape
    rank = factor.shape[1]
    count = scales.shape[0]
    steps = 4
    part = width // steps

    def columns(n):
        return pl.BlockSpec((n, part), lambda i: (0, i))

    def whole(a, b):
        return pl.BlockSpec((a, b), lambda i: (0, 0))

    def body(*refs):
        merge_kernel(width // count, *refs)

    return pl.pallas_call(
        body,
        grid=(steps,),
        in_specs=[columns(rows), whole(count, rows), whole(rows, rank), columns(rank)],
        out_specs=[columns(rows), columns(1)],
        out_shape=[
            jax.ShapeDtypeStruct((rows, width), BF),
            jax.ShapeDtypeStruct((1, width), F32),
        ],
        compiler_params=pltpu.CompilerParams(vmem_limit_bytes=60 * 1024 * 1024),
    )(codes, scales, factor, out_factor)


def tile_kernel(
    where, scaled, far_low, far_high, ratio, own, other, own_swap, other_swap, out, wide, far
):
    rows = own.shape[1]
    half = far_low.shape[0]
    x, zl, co = where[0], where[1], where[2]

    @pl.when(pl.program_id(0) == 0)
    def _():
        for source, base in ((far_low, 0), (far_high, half)):
            for r in range(0, half, 16):
                value = source[r : r + 16, :].astype(F32) * ratio[...]
                far[base + r : base + r + 16, :] = value.astype(BF)

    for source, zi, c in (
        (own, zl, co),
        (other, 1 - zl, co),
        (own_swap, zl, 1 - co),
        (other_swap, 1 - zl, 1 - co),
    ):
        row = pl.multiple_of((zi * 2 + c) * rows, rows)
        wide[pl.ds(row, rows), :] = source[0]

    def product(value):
        return lax.dot_general(
            value, wide[...], (((1,), (1,)), ((), ())), preferred_element_type=F32
        ).astype(BF)

    n = 2 * half
    tile = product(scaled[...])
    for k, e in enumerate((0, 3, 1)):
        out[lax.rem(x + e, 4), 0] = tile[k * n : (k + 1) * n, :]
    out[lax.rem(x + 2, 4), 0] = product(far[...])


def tile_of(where, scaled, far_low, far_high, ratio, weights):
    tokens, width = scaled.shape
    half = far_low.shape[0]
    n = 2 * half
    rows = weights[0].shape[1]

    def whole(shape):
        return pl.BlockSpec(shape, lambda i, w: (0, 0))

    weight = pl.BlockSpec((1, rows, width), lambda i, w: (i, 0, 0))
    return pl.pallas_call(
        tile_kernel,
        grid_spec=pltpu.PrefetchScalarGridSpec(
            num_scalar_prefetch=1,
            grid=(4,),
            in_specs=[whole((tokens, width)), whole((half, width)), whole((half, width))]
            + [whole((1, width))]
            + [weight] * 4,
            out_specs=pl.BlockSpec((4, 1, n, 4 * rows), lambda i, w: (0, i, 0, 0)),
            scratch_shapes=[pltpu.VMEM((4 * rows, width), BF), pltpu.VMEM((n, width), BF)],
        ),
        out_shape=jax.ShapeDtypeStruct((4, 4, n, 4 * rows), BF),
        compiler_params=pltpu.CompilerParams(vmem_limit_bytes=40 * 1024 * 1024),
        cost_estimate=pl.CostEstimate(
            flops=8 * n * 16 * rows * width,
            bytes_accessed=2 * width * (4 * n + 16 * rows),
            transcendentals=0,
        ),
    )(where, scaled, far_low, far_high, ratio, *weights)


def on_device(codes, scales, in_factor, out_factor, magnitude, inputs, grad, pre):
    y, x, zl, co, t = (lax.axis_index(a) for a in ("y", "x", "zl", "co", "t"))
    rows, width = codes.shape
    tokens = grad.shape[0]
    half = tokens // 2
    features = inputs.shape[1]
    part = features // SIZES["x"]
    rank = in_factor.shape[1]

    low_half, high_half = grad[:half], grad[half:]
    left_low, right_high = shift(low_half, "x", 1), shift(high_half, "x", -1)
    far_low, far_high = shift(left_low, "x", 1), shift(right_high, "x", -1)

    first = (((y * 4 + x) * 2 + zl) * 2 + co) * rows
    factor_rows = lax.dynamic_slice_in_dim(in_factor, first, rows, 0)
    own, squares = merge(codes, scales.T, factor_rows, out_factor)

    other = shift(own, "zl", 1)
    own_down, own_up = shift(own, "y", 1), shift(own, "y", -1)
    own_far = shift(after(own_down, left_low, right_high), "y", 1)
    other_down, other_up = shift(other, "y", 1), shift(other, "y", -1)
    other_far = shift(other_up, "y", -1)

    def in_order(blocks):
        buffer = jnp.zeros((4, rows, width), BF)
        for block, step in zip(blocks, (0, -1, 1, 2)):
            buffer = lax.dynamic_update_slice(buffer, block[None], ((y + step) % 4, 0, 0))
        return buffer

    own_rows = in_order((own, own_down, own_up, own_far))
    own_swap = shift(own_rows, "co", 1)
    other_rows = in_order((other, other_down, other_up, other_far))
    other_swap = shift(other_rows, "co", 1)

    total = squares.reshape(-1, 128)
    for axis in ("y", "x", "co", "zl"):
        steps = [shift(total, axis, k) for k in range(1, SIZES[axis])]
        for piece in steps:
            total = total + piece
        if axis == "x":
            left_high = shift(after(high_half, total), "x", 1)
            right_low = shift(after(low_half, total), "x", -1)
    col_norm = jnp.sqrt(total.reshape(-1) + 1e-06)
    ratio = magnitude / col_norm

    def scaled_of(g):
        return (g.astype(F32) * ratio).astype(BF)

    scaled_own = scaled_of(grad)
    scaled = scaled_of(
        jnp.concatenate([grad, left_low, left_high, right_low, right_high], axis=0)
    )

    factor_cols = lax.dynamic_slice_in_dim(in_factor, t * features, features, 0)
    hidden = jnp.dot(inputs, factor_cols, preferred_element_type=F32)
    back = lax.dot_general(
        scaled_own, out_factor, (((1,), (1,)), ((), ())), preferred_element_type=F32
    )
    low = jnp.concatenate([hidden, back], axis=1).astype(BF)
    low = after(low, own_far, other_down, other_up)
    pieces = [shift(low, "t", k) for k in (1, 2, 3)]
    low = sum((p.astype(F32) for p in pieces), low.astype(F32)).astype(BF)
    hidden, back = low[:, :rank], low[:, rank:]
    in_grad = SCALE * lax.dot_general(
        back, inputs, (((0,), (0,)), ((), ())), preferred_element_type=F32
    )
    out_grad = SCALE * lax.dot_general(
        hidden, scaled_own, (((0,), (0,)), ((), ())), preferred_element_type=F32
    )
    mag_sum = jnp.sum(grad.astype(F32) * pre.astype(F32), axis=0).reshape(N_DP, -1)
    adapters = jnp.concatenate([out_grad, in_grad, mag_sum], axis=1)
    adapters = after(adapters, other_far)
    side = adapters.shape[0] // 2
    keep = lax.dynamic_slice_in_dim(adapters, co * side, side, 0)
    give = lax.dynamic_slice_in_dim(adapters, (1 - co) * side, side, 0)
    adapters = keep + shift(give, "co", 1)
    adapters = after(adapters, left_high, right_low).reshape(16, 2, -1)
    keep = lax.dynamic_index_in_dim(adapters, zl, 1, False)
    give = lax.dynamic_index_in_dim(adapters, 1 - zl, 1, False)
    adapters = swap_all(keep + shift(give, "zl", 1), ("y", "x"))
    adapters = jnp.sum(adapters, axis=0)
    columns = adapters.shape[0]
    across = shift(adapters.reshape(-1, 8), "zl", 1).reshape(-1)
    adapters = jnp.where(
        zl == 0,
        jnp.concatenate([adapters, across]),
        jnp.concatenate([across, adapters]),
    )
    adapters = after(adapters, far_low, far_high)
    adapters = swap_all(jnp.broadcast_to(adapters[None], (16, 2 * columns)), ("y", "x"))
    adapters = adapters.reshape(-1, columns)
    across = shift(adapters, "co", 1)
    adapters = jnp.where(
        co == 0, jnp.stack([adapters, across]), jnp.stack([across, adapters])
    ).reshape(N_DP, -1)
    out_grad = adapters[:, :width]
    in_grad = adapters[:, width : width + features].T
    mag_grad = adapters[:, width + features :].reshape(-1) / col_norm

    where = jnp.stack([x, zl, co]).astype(jnp.int32)
    weights = (own_rows, other_rows, own_swap, other_swap)
    tile = tile_of(where, scaled, far_low, far_high, ratio.reshape(1, -1), weights)
    tile = swap_all(tile.reshape(16, tokens, part), ("x", "t"))

    tile = jnp.sum(tile.reshape(4, 4, tokens, part).astype(F32), axis=1).astype(BF)
    grad_in = tile.transpose(1, 0, 2).reshape(tokens, features)
    return grad_in, in_grad, out_grad, mag_grad


def solution(mesh):
    fine = Mesh(mesh.devices.reshape(4, 4, 2, 2, 4), ("y", "x", "zl", "co", "t"))
    in_specs = (
        P(DP, "t"),
        P(DP, "t"),
        P(),
        P(None, "t"),
        P("t"),
        P(DP, "t"),
        P(DP, "t"),
        P(DP, "t"),
    )
    out_specs = (P(DP, "t"), P("t", None), P(None, "t"), P("t"))
    return jax.shard_map(
        on_device, mesh=fine, in_specs=in_specs, out_specs=out_specs, check_vma=False
    )
```

```python
import jax
import jax.numpy as jnp
from jax import lax
from jax.experimental import pallas as pl
from jax.experimental.pallas import tpu as pltpu
from jax.sharding import Mesh, PartitionSpec as P

SCALE = 0.5
BF = jnp.bfloat16
F32 = jnp.float32
SIZES = {"y": 4, "x": 4, "zl": 2, "co": 2, "t": 4}
DP = ("y", "x", "zl", "co")
N_DP = 64


def shift(value, axis, step):
    n = SIZES[axis]
    return lax.ppermute(value, axis, [(i, (i + step) % n) for i in range(n)])


def swap_all(value, axes):
    return lax.all_to_all(value, axes, 0, 0, tiled=True)


def after(value, *earlier):
    return lax.optimization_barrier((value,) + earlier)[0]


def merge_kernel(block, codes, scales, factor, out_factor, own, squares):
    width = codes.shape[1]
    count = scales.shape[0]
    start = pl.program_id(0) * width
    group = (start + lax.broadcasted_iota(jnp.int32, (count, width), 1)) // block
    pick = (group == lax.broadcasted_iota(jnp.int32, (count, width), 0)).astype(F32)
    spread = lax.dot_general(
        scales[...],
        pick,
        (((0,), (0,)), ((), ())),
        precision=lax.Precision.HIGHEST,
        preferred_element_type=F32,
    )
    low = jnp.dot(factor[...], out_factor[...], preferred_element_type=F32)
    merged = ((codes[...].astype(F32) - 7.5) * spread + SCALE * low).astype(BF)
    own[...] = merged
    wide = merged.astype(F32)
    squares[...] = jnp.sum(wide * wide, axis=0, keepdims=True)


def merge(codes, scales, factor, out_factor):
    rows, width = codes.shape
    rank = factor.shape[1]
    count = scales.shape[0]
    steps = 4
    part = width // steps

    def columns(n):
        return pl.BlockSpec((n, part), lambda i: (0, i))

    def whole(a, b):
        return pl.BlockSpec((a, b), lambda i: (0, 0))

    def body(*refs):
        merge_kernel(width // count, *refs)

    return pl.pallas_call(
        body,
        grid=(steps,),
        in_specs=[columns(rows), whole(count, rows), whole(rows, rank), columns(rank)],
        out_specs=[columns(rows), columns(1)],
        out_shape=[
            jax.ShapeDtypeStruct((rows, width), BF),
            jax.ShapeDtypeStruct((1, width), F32),
        ],
        compiler_params=pltpu.CompilerParams(vmem_limit_bytes=60 * 1024 * 1024),
    )(codes, scales, factor, out_factor)


def tile_kernel(
    where, scaled, far_low, far_high, ratio, own, other, own_swap, other_swap, out, wide, far
):
    rows = own.shape[1]
    half = far_low.shape[0]
    x, zl, co = where[0], where[1], where[2]

    @pl.when(pl.program_id(0) == 0)
    def _():
        for source, base in ((far_low, 0), (far_high, half)):
            for r in range(0, half, 16):
                value = source[r : r + 16, :].astype(F32) * ratio[...]
                far[base + r : base + r + 16, :] = value.astype(BF)

    for source, zi, c in (
        (own, zl, co),
        (other, 1 - zl, co),
        (own_swap, zl, 1 - co),
        (other_swap, 1 - zl, 1 - co),
    ):
        row = pl.multiple_of((zi * 2 + c) * rows, rows)
        wide[pl.ds(row, rows), :] = source[0]

    def product(value):
        return lax.dot_general(
            value, wide[...], (((1,), (1,)), ((), ())), preferred_element_type=F32
        ).astype(BF)

    n = 2 * half
    tile = product(scaled[...])
    for k, e in enumerate((0, 3, 1)):
        out[lax.rem(x + e, 4), 0] = tile[k * n : (k + 1) * n, :]
    out[lax.rem(x + 2, 4), 0] = product(far[...])


def tile_of(where, scaled, far_low, far_high, ratio, weights):
    tokens, width = scaled.shape
    half = far_low.shape[0]
    n = 2 * half
    rows = weights[0].shape[1]

    def place(i, where):
        step = jnp.where(i == 0, 0, jnp.where(i == 1, 3, i - 1))
        return 0, lax.rem(where[3] + step, 4), 0, 0

    def whole(shape):
        return pl.BlockSpec(shape, lambda i, w: (0, 0))

    weight = pl.BlockSpec((1, rows, width), lambda i, w: (i, 0, 0))
    return pl.pallas_call(
        tile_kernel,
        grid_spec=pltpu.PrefetchScalarGridSpec(
            num_scalar_prefetch=1,
            grid=(4,),
            in_specs=[whole((tokens, width)), whole((half, width)), whole((half, width))]
            + [whole((1, width))]
            + [weight] * 4,
            out_specs=pl.BlockSpec((4, 1, n, 4 * rows), place),
            scratch_shapes=[pltpu.VMEM((4 * rows, width), BF), pltpu.VMEM((n, width), BF)],
        ),
        out_shape=jax.ShapeDtypeStruct((4, 4, n, 4 * rows), BF),
        compiler_params=pltpu.CompilerParams(vmem_limit_bytes=40 * 1024 * 1024),
        cost_estimate=pl.CostEstimate(
            flops=8 * n * 16 * rows * width,
            bytes_accessed=2 * width * (4 * n + 16 * rows),
            transcendentals=0,
        ),
    )(where, scaled, far_low, far_high, ratio, *weights)


def on_device(codes, scales, in_factor, out_factor, magnitude, inputs, grad, pre):
    y, x, zl, co, t = (lax.axis_index(a) for a in ("y", "x", "zl", "co", "t"))
    rows, width = codes.shape
    tokens = grad.shape[0]
    half = tokens // 2
    features = inputs.shape[1]
    part = features // SIZES["x"]
    rank = in_factor.shape[1]

    def gather_sum(value, axis):
        steps = [shift(value, axis, k) for k in range(1, SIZES[axis])]
        for piece in steps:
            value = value + piece
        return value

    first = (((y * 4 + x) * 2 + zl) * 2 + co) * rows
    factor_rows = lax.dynamic_slice_in_dim(in_factor, first, rows, 0)
    own, squares = merge(codes, scales.T, factor_rows, out_factor)

    low_half, high_half = grad[:half], grad[half:]
    left_low, right_high = shift(low_half, "x", 1), shift(high_half, "x", -1)
    other = shift(own, "zl", 1)
    own_down, own_up = shift(own, "y", 1), shift(own, "y", -1)
    total = gather_sum(gather_sum(squares.reshape(-1, 128), "y"), "co")
    phase = (left_low, right_high, other, own_down, own_up, total, low_half, high_half)
    phase = lax.optimization_barrier(phase)
    left_low, right_high, other, own_down, own_up, total, low_half, high_half = phase

    left_high, right_low = shift(high_half, "x", 1), shift(low_half, "x", -1)
    other_down, other_up = shift(other, "y", 1), shift(other, "y", -1)
    own_far = shift(own_down, "y", 1)
    total = after(gather_sum(total, "zl"), other_down, other_up, own_far)
    total = gather_sum(total, "x")
    phase = (left_low, right_high, left_high, right_low, other_down, other_up, own_far, total)
    phase = lax.optimization_barrier(phase)
    left_low, right_high, left_high, right_low, other_down, other_up, own_far, total = phase

    far_low, far_high = shift(left_low, "x", 1), shift(right_high, "x", -1)
    other_far = shift(other_up, "y", -1)
    own_rows = jnp.stack([own, own_down, own_up, own_far])
    own_swap = shift(own_rows, "co", 1)
    other_rows = jnp.stack([other, other_down, other_up, other_far])
    other_swap = shift(other_rows, "co", 1)
    col_norm = jnp.sqrt(total.reshape(-1) + 1e-06)
    ratio = magnitude / col_norm

    def scaled_of(g):
        return (g.astype(F32) * ratio).astype(BF)

    scaled_own = scaled_of(grad)
    scaled = scaled_of(
        jnp.concatenate([grad, left_low, left_high, right_low, right_high], axis=0)
    )

    factor_cols = lax.dynamic_slice_in_dim(in_factor, t * features, features, 0)
    hidden = jnp.dot(inputs, factor_cols, preferred_element_type=F32)
    back = lax.dot_general(
        scaled_own, out_factor, (((1,), (1,)), ((), ())), preferred_element_type=F32
    )
    low = jnp.concatenate([hidden, back], axis=1).astype(BF)
    pieces = [shift(low, "t", k) for k in (1, 2, 3)]
    low = sum((p.astype(F32) for p in pieces), low.astype(F32)).astype(BF)
    low = after(low, far_low, far_high, other_far)
    hidden, back = low[:, :rank], low[:, rank:]
    in_grad = SCALE * lax.dot_general(
        back, inputs, (((0,), (0,)), ((), ())), preferred_element_type=F32
    )
    out_grad = SCALE * lax.dot_general(
        hidden, scaled_own, (((0,), (0,)), ((), ())), preferred_element_type=F32
    )
    mag_sum = jnp.sum(grad.astype(F32) * pre.astype(F32), axis=0).reshape(N_DP, -1)
    adapters = jnp.concatenate([out_grad, in_grad, mag_sum], axis=1)
    side = adapters.shape[0] // 2
    keep = lax.dynamic_slice_in_dim(adapters, co * side, side, 0)
    give = lax.dynamic_slice_in_dim(adapters, (1 - co) * side, side, 0)
    adapters = keep + shift(give, "co", 1)
    for axis, index in (("y", y), ("x", x)):
        side = adapters.shape[0] // 4
        total = lax.dynamic_slice_in_dim(adapters, index * side, side, 0)
        for k in (1, 2, 3):
            give = lax.dynamic_slice_in_dim(adapters, ((index + k) % 4) * side, side, 0)
            total = total + shift(give, axis, k)
        adapters = total
    adapters = adapters + shift(adapters, "zl", 1)

    where = jnp.stack([x, zl, co, y]).astype(jnp.int32)
    weights = (own_rows, other_rows, own_swap, other_swap)
    tile = tile_of(where, scaled, far_low, far_high, ratio.reshape(1, -1), weights)
    adapters = after(adapters, tile)
    tile = swap_all(tile.reshape(16, tokens, part), ("x", "t"))

    for axis, index in (("x", x), ("y", y), ("co", co)):
        n = SIZES[axis]
        side = adapters.shape[0]
        total = jnp.zeros((n * side, adapters.shape[1]), F32)
        for k in range(n):
            got = shift(adapters, axis, k) if k else adapters
            total = lax.dynamic_update_slice(total, got, (((index - k) % n) * side, 0))
        adapters = total
    out_grad = adapters[:, :width]
    in_grad = adapters[:, width : width + features].T
    mag_grad = adapters[:, width + features :].reshape(-1) / col_norm

    tile = jnp.sum(tile.reshape(4, 4, tokens, part).astype(F32), axis=1).astype(BF)
    grad_in = tile.transpose(1, 0, 2).reshape(tokens, features)
    return grad_in, in_grad, out_grad, mag_grad


def solution(mesh):
    fine = Mesh(mesh.devices.reshape(4, 4, 2, 2, 4), ("y", "x", "zl", "co", "t"))
    in_specs = (
        P(DP, "t"),
        P(DP, "t"),
        P(),
        P(None, "t"),
        P("t"),
        P(DP, "t"),
        P(DP, "t"),
        P(DP, "t"),
    )
    out_specs = (P(DP, "t"), P("t", None), P(None, "t"), P("t"))
    return jax.shard_map(
        on_device, mesh=fine, in_specs=in_specs, out_specs=out_specs, check_vma=False
    )
```

```python
import jax
import jax.numpy as jnp
from jax import lax
from jax.experimental import pallas as pl
from jax.experimental.pallas import tpu as pltpu
from jax.sharding import Mesh, PartitionSpec as P

SCALE = 0.5
BF = jnp.bfloat16
F32 = jnp.float32
SIZES = {"y": 4, "x": 4, "zl": 2, "co": 2, "t": 4}
DP = ("y", "x", "zl", "co")
N_DP = 64


def shift(value, axis, step):
    n = SIZES[axis]
    return lax.ppermute(value, axis, [(i, (i + step) % n) for i in range(n)])


def swap_all(value, axes):
    return lax.all_to_all(value, axes, 0, 0, tiled=True)


def after(value, *earlier):
    return lax.optimization_barrier((value,) + earlier)[0]


def merge_kernel(block, codes, scales, factor, out_factor, own, squares):
    width = codes.shape[1]
    count = scales.shape[0]
    start = pl.program_id(0) * width
    group = (start + lax.broadcasted_iota(jnp.int32, (count, width), 1)) // block
    pick = (group == lax.broadcasted_iota(jnp.int32, (count, width), 0)).astype(F32)
    spread = lax.dot_general(
        scales[...],
        pick,
        (((0,), (0,)), ((), ())),
        precision=lax.Precision.HIGHEST,
        preferred_element_type=F32,
    )
    low = jnp.dot(factor[...], out_factor[...], preferred_element_type=F32)
    merged = ((codes[...].astype(F32) - 7.5) * spread + SCALE * low).astype(BF)
    own[...] = merged
    wide = merged.astype(F32)
    squares[...] = jnp.sum(wide * wide, axis=0, keepdims=True)


def merge(codes, scales, factor, out_factor):
    rows, width = codes.shape
    rank = factor.shape[1]
    count = scales.shape[0]
    steps = 4
    part = width // steps

    def columns(n):
        return pl.BlockSpec((n, part), lambda i: (0, i))

    def whole(a, b):
        return pl.BlockSpec((a, b), lambda i: (0, 0))

    def body(*refs):
        merge_kernel(width // count, *refs)

    return pl.pallas_call(
        body,
        grid=(steps,),
        in_specs=[columns(rows), whole(count, rows), whole(rows, rank), columns(rank)],
        out_specs=[columns(rows), columns(1)],
        out_shape=[
            jax.ShapeDtypeStruct((rows, width), BF),
            jax.ShapeDtypeStruct((1, width), F32),
        ],
        compiler_params=pltpu.CompilerParams(vmem_limit_bytes=60 * 1024 * 1024),
    )(codes, scales, factor, out_factor)


def tile_kernel(
    where, scaled, far_low, far_high, ratio, own, other, own_swap, other_swap, first, second, wide, far
):
    rows = own.shape[1]
    half = far_low.shape[0]
    x, zl, co = where[0], where[1], where[2]

    @pl.when(pl.program_id(0) == 0)
    def _():
        for source, base in ((far_low, 0), (far_high, half)):
            for r in range(0, half, 16):
                value = source[r : r + 16, :].astype(F32) * ratio[...]
                far[base + r : base + r + 16, :] = value.astype(BF)

    for source, zi, c in (
        (own, zl, co),
        (other, 1 - zl, co),
        (own_swap, zl, 1 - co),
        (other_swap, 1 - zl, 1 - co),
    ):
        row = pl.multiple_of((zi * 2 + c) * rows, rows)
        wide[pl.ds(row, rows), :] = source[0]

    def product(value):
        return lax.dot_general(
            value, wide[...], (((1,), (1,)), ((), ())), preferred_element_type=F32
        ).astype(BF)

    n = 2 * half
    tile = product(scaled[...])
    for k, e in enumerate((0, 3, 1)):
        first[lax.rem(x + e, 4), 0] = tile[k * n : k * n + half, :]
        second[lax.rem(x + e, 4), 0] = tile[k * n + half : (k + 1) * n, :]
    tile = product(far[...])
    first[lax.rem(x + 2, 4), 0] = tile[:half, :]
    second[lax.rem(x + 2, 4), 0] = tile[half:, :]


def tile_of(where, scaled, far_low, far_high, ratio, weights):
    tokens, width = scaled.shape
    half = far_low.shape[0]
    n = 2 * half
    rows = weights[0].shape[1]

    def place(i, where):
        step = jnp.where(i == 0, 0, jnp.where(i == 1, 3, i - 1))
        return 0, lax.rem(where[3] + step, 4), 0, 0

    def whole(shape):
        return pl.BlockSpec(shape, lambda i, w: (0, 0))

    weight = pl.BlockSpec((1, rows, width), lambda i, w: (i, 0, 0))
    return pl.pallas_call(
        tile_kernel,
        grid_spec=pltpu.PrefetchScalarGridSpec(
            num_scalar_prefetch=1,
            grid=(4,),
            in_specs=[whole((tokens, width)), whole((half, width)), whole((half, width))]
            + [whole((1, width))]
            + [weight] * 4,
            out_specs=[pl.BlockSpec((4, 1, half, 4 * rows), place)] * 2,
            scratch_shapes=[pltpu.VMEM((4 * rows, width), BF), pltpu.VMEM((n, width), BF)],
        ),
        out_shape=[jax.ShapeDtypeStruct((4, 4, half, 4 * rows), BF)] * 2,
        compiler_params=pltpu.CompilerParams(vmem_limit_bytes=40 * 1024 * 1024),
        cost_estimate=pl.CostEstimate(
            flops=8 * n * 16 * rows * width,
            bytes_accessed=2 * width * (4 * n + 16 * rows),
            transcendentals=0,
        ),
    )(where, scaled, far_low, far_high, ratio, *weights)


def on_device(codes, scales, in_factor, out_factor, magnitude, inputs, grad, pre):
    y, x, zl, co, t = (lax.axis_index(a) for a in ("y", "x", "zl", "co", "t"))
    rows, width = codes.shape
    tokens = grad.shape[0]
    half = tokens // 2
    features = inputs.shape[1]
    part = features // SIZES["x"]
    rank = in_factor.shape[1]

    def gather_sum(value, axis):
        steps = [shift(value, axis, k) for k in range(1, SIZES[axis])]
        for piece in steps:
            value = value + piece
        return value

    first = (((y * 4 + x) * 2 + zl) * 2 + co) * rows
    factor_rows = lax.dynamic_slice_in_dim(in_factor, first, rows, 0)
    own, squares = merge(codes, scales.T, factor_rows, out_factor)

    low_half, high_half = grad[:half], grad[half:]
    left_low, right_high = shift(low_half, "x", 1), shift(high_half, "x", -1)
    other = shift(own, "zl", 1)
    own_down, own_up = shift(own, "y", 1), shift(own, "y", -1)
    total = gather_sum(gather_sum(squares.reshape(-1, 128), "x"), "y")
    phase = (left_low, right_high, other, own_down, own_up, total, low_half, high_half)
    phase = lax.optimization_barrier(phase)
    left_low, right_high, other, own_down, own_up, total, low_half, high_half = phase

    left_high, right_low = shift(high_half, "x", 1), shift(low_half, "x", -1)
    other_down, other_up = shift(other, "y", 1), shift(other, "y", -1)
    own_far = shift(own_down, "y", 1)
    total = gather_sum(gather_sum(total, "co"), "zl")
    phase = (left_low, right_high, left_high, right_low, other_down, other_up, own_far, total)
    phase = lax.optimization_barrier(phase)
    left_low, right_high, left_high, right_low, other_down, other_up, own_far, total = phase

    far_low, far_high = shift(left_low, "x", 1), shift(right_high, "x", -1)
    other_far = shift(other_up, "y", -1)
    col_norm = jnp.sqrt(total.reshape(-1) + 1e-06)
    ratio = magnitude / col_norm

    def scaled_of(g):
        return (g.astype(F32) * ratio).astype(BF)

    scaled_own = scaled_of(grad)
    scaled = scaled_of(
        jnp.concatenate([grad, left_low, left_high, right_low, right_high], axis=0)
    )

    factor_cols = lax.dynamic_slice_in_dim(in_factor, t * features, features, 0)
    hidden = jnp.dot(inputs, factor_cols, preferred_element_type=F32)
    back = lax.dot_general(
        scaled_own, out_factor, (((1,), (1,)), ((), ())), preferred_element_type=F32
    )
    low = jnp.concatenate([hidden, back], axis=1).astype(BF)
    pieces = [shift(low, "t", k) for k in (1, 2, 3)]
    low = sum((p.astype(F32) for p in pieces), low.astype(F32)).astype(BF)
    hidden, back = low[:, :rank], low[:, rank:]
    in_grad = SCALE * lax.dot_general(
        back, inputs, (((0,), (0,)), ((), ())), preferred_element_type=F32
    )
    out_grad = SCALE * lax.dot_general(
        hidden, scaled_own, (((0,), (0,)), ((), ())), preferred_element_type=F32
    )
    mag_sum = jnp.sum(grad.astype(F32) * pre.astype(F32), axis=0).reshape(N_DP, -1)
    adapters = jnp.concatenate([out_grad, in_grad, mag_sum], axis=1)
    phase = lax.optimization_barrier((far_low, far_high, other_far, adapters))
    far_low, far_high, other_far, adapters = phase
    own_rows = jnp.stack([own, own_down, own_up, own_far])
    own_swap = shift(own_rows, "co", 1)
    other_rows = jnp.stack([other, other_down, other_up, other_far])
    other_swap = shift(other_rows, "co", 1)
    side = adapters.shape[0] // 2
    keep = lax.dynamic_slice_in_dim(adapters, co * side, side, 0)
    give = lax.dynamic_slice_in_dim(adapters, (1 - co) * side, side, 0)
    adapters = keep + shift(give, "co", 1)
    adapters = adapters + shift(adapters, "zl", 1)

    where = jnp.stack([x, zl, co, y]).astype(jnp.int32)
    weights = (own_rows, other_rows, own_swap, other_swap)
    tiles = tile_of(where, scaled, far_low, far_high, ratio.reshape(1, -1), weights)
    adapters = after(adapters, tiles[0])
    tiles = [swap_all(v.reshape(16, half, part), ("x", "t")) for v in tiles]

    for axis, index in (("y", y), ("x", x)):
        side = adapters.shape[0] // 4
        total = lax.dynamic_slice_in_dim(adapters, index * side, side, 0)
        for k in (1, 2, 3):
            give = lax.dynamic_slice_in_dim(adapters, ((index + k) % 4) * side, side, 0)
            total = total + shift(give, axis, k)
        adapters = total
    adapters = after(adapters, tiles[0])
    for axis, index in (("x", x), ("y", y), ("co", co)):
        if axis == "co":
            tiles[1] = after(tiles[1], adapters)
        n = SIZES[axis]
        side = adapters.shape[0]
        total = jnp.zeros((n * side, adapters.shape[1]), F32)
        for k in range(n):
            got = shift(adapters, axis, k) if k else adapters
            total = lax.dynamic_update_slice(total, got, (((index - k) % n) * side, 0))
        adapters = total
    out_grad = adapters[:, :width]
    in_grad = adapters[:, width : width + features].T
    mag_grad = adapters[:, width + features :].reshape(-1) / col_norm

    tiles = [jnp.sum(v.reshape(4, 4, half, part).astype(F32), axis=1).astype(BF) for v in tiles]
    grad_in = jnp.concatenate(
        [v.transpose(1, 0, 2).reshape(half, features) for v in tiles], axis=0
    )
    return grad_in, in_grad, out_grad, mag_grad


def solution(mesh):
    fine = Mesh(mesh.devices.reshape(4, 4, 2, 2, 4), ("y", "x", "zl", "co", "t"))
    in_specs = (
        P(DP, "t"),
        P(DP, "t"),
        P(),
        P(None, "t"),
        P("t"),
        P(DP, "t"),
        P(DP, "t"),
        P(DP, "t"),
    )
    out_specs = (P(DP, "t"), P("t", None), P(None, "t"), P("t"))
    return jax.shard_map(
        on_device, mesh=fine, in_specs=in_specs, out_specs=out_specs, check_vma=False
    )
```

```python
import jax
import jax.numpy as jnp
from jax import lax
from jax.experimental import pallas as pl
from jax.experimental.pallas import tpu as pltpu
from jax.sharding import Mesh, PartitionSpec as P

SCALE = 0.5
BF = jnp.bfloat16
F32 = jnp.float32
SIZES = {"y": 4, "x": 4, "zl": 2, "co": 2, "t": 4, ("zl", "co"): 4}
DP = ("y", "x", "zl", "co")
N_DP = 64


def shift(value, axis, step):
    n = SIZES[axis]
    return lax.ppermute(value, axis, [(i, (i + step) % n) for i in range(n)])


def swap_all(value, axes):
    return lax.all_to_all(value, axes, 0, 0, tiled=True)


def after(value, *earlier):
    return lax.optimization_barrier((value,) + earlier)[0]


def merge_kernel(block, codes, scales, factor, out_factor, own, squares):
    width = codes.shape[1]
    count = scales.shape[0]
    start = pl.program_id(0) * width
    group = (start + lax.broadcasted_iota(jnp.int32, (count, width), 1)) // block
    pick = (group == lax.broadcasted_iota(jnp.int32, (count, width), 0)).astype(F32)
    spread = lax.dot_general(
        scales[...],
        pick,
        (((0,), (0,)), ((), ())),
        precision=lax.Precision.HIGHEST,
        preferred_element_type=F32,
    )
    low = jnp.dot(factor[...], out_factor[...], preferred_element_type=F32)
    merged = ((codes[...].astype(F32) - 7.5) * spread + SCALE * low).astype(BF)
    own[...] = merged
    wide = merged.astype(F32)
    squares[...] = jnp.sum(wide * wide, axis=0, keepdims=True)


def merge(codes, scales, factor, out_factor):
    rows, width = codes.shape
    rank = factor.shape[1]
    count = scales.shape[0]
    steps = 4
    part = width // steps

    def columns(n):
        return pl.BlockSpec((n, part), lambda i: (0, i))

    def whole(a, b):
        return pl.BlockSpec((a, b), lambda i: (0, 0))

    def body(*refs):
        merge_kernel(width // count, *refs)

    return pl.pallas_call(
        body,
        grid=(steps,),
        in_specs=[columns(rows), whole(count, rows), whole(rows, rank), columns(rank)],
        out_specs=[columns(rows), columns(1)],
        out_shape=[
            jax.ShapeDtypeStruct((rows, width), BF),
            jax.ShapeDtypeStruct((1, width), F32),
        ],
        compiler_params=pltpu.CompilerParams(vmem_limit_bytes=60 * 1024 * 1024),
        cost_estimate=pl.CostEstimate(
            flops=2 * rows * width * (rank + 8 * count),
            bytes_accessed=8 * rows * width,
            transcendentals=0,
        ),
    )(codes, scales, factor, out_factor)


def tile_kernel(
    where, scaled, far_low, far_high, ratio, own, other, own_swap, other_swap, out, wide, far
):
    rows = own.shape[1]
    half = far_low.shape[0]
    x, zl, co = where[0], where[1], where[2]

    @pl.when(pl.program_id(0) == 0)
    def _():
        for source, base in ((far_low, 0), (far_high, half)):
            for r in range(0, half, 16):
                value = source[r : r + 16, :].astype(F32) * ratio[...]
                far[base + r : base + r + 16, :] = value.astype(BF)

    for source, zi, c in (
        (own, zl, co),
        (other, 1 - zl, co),
        (own_swap, zl, 1 - co),
        (other_swap, 1 - zl, 1 - co),
    ):
        row = pl.multiple_of((zi * 2 + c) * rows, rows)
        wide[pl.ds(row, rows), :] = source[0]

    def product(value):
        return lax.dot_general(
            value, wide[...], (((1,), (1,)), ((), ())), preferred_element_type=F32
        ).astype(BF)

    n = 2 * half
    tile = product(scaled[...])
    for k, e in enumerate((0, 3, 1)):
        out[lax.rem(x + e, 4), 0] = tile[k * n : (k + 1) * n, :]
    out[lax.rem(x + 2, 4), 0] = product(far[...])


def tile_of(where, scaled, far_low, far_high, ratio, weights):
    tokens, width = scaled.shape
    half = far_low.shape[0]
    n = 2 * half
    rows = weights[0].shape[1]

    def place(i, where):
        step = jnp.where(i == 0, 0, jnp.where(i == 1, 3, i - 1))
        return 0, lax.rem(where[3] + step, 4), 0, 0

    def whole(shape):
        return pl.BlockSpec(shape, lambda i, w: (0, 0))

    weight = pl.BlockSpec((1, rows, width), lambda i, w: (i, 0, 0))
    return pl.pallas_call(
        tile_kernel,
        grid_spec=pltpu.PrefetchScalarGridSpec(
            num_scalar_prefetch=1,
            grid=(4,),
            in_specs=[whole((tokens, width)), whole((half, width)), whole((half, width))]
            + [whole((1, width))]
            + [weight] * 4,
            out_specs=pl.BlockSpec((4, 1, n, 4 * rows), place),
            scratch_shapes=[pltpu.VMEM((4 * rows, width), BF), pltpu.VMEM((n, width), BF)],
        ),
        out_shape=jax.ShapeDtypeStruct((4, 4, n, 4 * rows), BF),
        compiler_params=pltpu.CompilerParams(vmem_limit_bytes=40 * 1024 * 1024),
        cost_estimate=pl.CostEstimate(
            flops=8 * n * 16 * rows * width,
            bytes_accessed=2 * width * (4 * n + 16 * rows),
            transcendentals=0,
        ),
    )(where, scaled, far_low, far_high, ratio, *weights)


def on_device(codes, scales, in_factor, out_factor, magnitude, inputs, grad, pre):
    y, x, zl, co, t = (lax.axis_index(a) for a in ("y", "x", "zl", "co", "t"))
    rows, width = codes.shape
    tokens = grad.shape[0]
    half = tokens // 2
    features = inputs.shape[1]
    part = features // SIZES["x"]
    rank = in_factor.shape[1]

    def gather_sum(value, axis):
        steps = [shift(value, axis, k) for k in range(1, SIZES[axis])]
        for piece in steps:
            value = value + piece
        return value

    first = (((y * 4 + x) * 2 + zl) * 2 + co) * rows
    factor_rows = lax.dynamic_slice_in_dim(in_factor, first, rows, 0)
    own, squares = merge(codes, scales.T, factor_rows, out_factor)

    low_half, high_half = grad[:half], grad[half:]
    left_low, right_high = shift(low_half, "x", 1), shift(high_half, "x", -1)
    other = shift(own, "zl", 1)
    own_down, own_up = shift(own, "y", 1), shift(own, "y", -1)
    total = gather_sum(squares.reshape(-1, 128), "y")
    phase = (left_low, right_high, other, own_down, own_up, total, low_half, high_half)
    phase = lax.optimization_barrier(phase)
    left_low, right_high, other, own_down, own_up, total, low_half, high_half = phase

    left_high, right_low = shift(high_half, "x", 1), shift(low_half, "x", -1)
    other_down, other_up = shift(other, "y", 1), shift(other, "y", -1)
    total = gather_sum(gather_sum(total, "x"), ("zl", "co"))
    phase = (left_low, right_high, left_high, right_low, other_down, other_up, own_down, total)
    phase = lax.optimization_barrier(phase)
    left_low, right_high, left_high, right_low, other_down, other_up, own_down, total = phase

    far_low, far_high = shift(left_low, "x", 1), shift(right_high, "x", -1)
    own_far = shift(own_down, "y", 1)
    other_far = shift(other_up, "y", -1)
    col_norm = jnp.sqrt(total.reshape(-1) + 1e-06)
    ratio = magnitude / col_norm

    def scaled_of(g):
        return (g.astype(F32) * ratio).astype(BF)

    scaled_own = scaled_of(grad)
    scaled = scaled_of(
        jnp.concatenate([grad, left_low, left_high, right_low, right_high], axis=0)
    )

    factor_cols = lax.dynamic_slice_in_dim(in_factor, t * features, features, 0)
    hidden = jnp.dot(inputs, factor_cols, preferred_element_type=F32)
    back = lax.dot_general(
        scaled_own, out_factor, (((1,), (1,)), ((), ())), preferred_element_type=F32
    )
    low = jnp.concatenate([hidden, back], axis=1).astype(BF)
    pieces = [shift(low, "t", k) for k in (1, 2, 3)]
    low = sum((p.astype(F32) for p in pieces), low.astype(F32)).astype(BF)
    hidden, back = low[:, :rank], low[:, rank:]
    in_grad = SCALE * lax.dot_general(
        back, inputs, (((0,), (0,)), ((), ())), preferred_element_type=F32
    )
    out_grad = SCALE * lax.dot_general(
        hidden, scaled_own, (((0,), (0,)), ((), ())), preferred_element_type=F32
    )
    mag_sum = jnp.sum(grad.astype(F32) * pre.astype(F32), axis=0).reshape(N_DP, -1)
    adapters = jnp.concatenate([out_grad, in_grad, mag_sum], axis=1)
    phase = (far_low, far_high, own_far, other_far, adapters, scaled)
    phase = lax.optimization_barrier(phase)
    far_low, far_high, own_far, other_far, adapters, scaled = phase
    own_rows = jnp.stack([own, own_down, own_up, own_far])
    own_swap = shift(own_rows, "co", 1)
    other_rows = jnp.stack([other, other_down, other_up, other_far])
    other_swap = shift(other_rows, "co", 1)
    columns = adapters.shape[1]
    adapters = swap_all(adapters.reshape(N_DP // 2, -1), ("y", "x", "co"))

    where = jnp.stack([x, zl, co, y]).astype(jnp.int32)
    weights = (own_rows, other_rows, own_swap, other_swap)
    tile = tile_of(where, scaled, far_low, far_high, ratio.reshape(1, -1), weights)
    adapters = jnp.sum(adapters, axis=0).reshape(-1, columns)
    adapters = adapters + shift(adapters, "zl", 1)
    tile = swap_all(after(tile, adapters).reshape(16, tokens, part), ("x", "t"))

    for axis, index in (("co", co), ("x", x), ("y", y)):
        n = SIZES[axis]
        side = adapters.shape[0]
        total = jnp.zeros((n * side, columns), F32)
        for k in range(n):
            got = shift(adapters, axis, k) if k else adapters
            total = lax.dynamic_update_slice(total, got, (((index - k) % n) * side, 0))
        adapters = total
    out_grad = adapters[:, :width]
    in_grad = adapters[:, width : width + features].T
    mag_grad = adapters[:, width + features :].reshape(-1) / col_norm

    tile = jnp.sum(tile.reshape(4, 4, tokens, part).astype(F32), axis=1).astype(BF)
    grad_in = tile.transpose(1, 0, 2).reshape(tokens, features)
    return grad_in, in_grad, out_grad, mag_grad


def solution(mesh):
    fine = Mesh(mesh.devices.reshape(4, 4, 2, 2, 4), ("y", "x", "zl", "co", "t"))
    in_specs = (
        P(DP, "t"),
        P(DP, "t"),
        P(),
        P(None, "t"),
        P("t"),
        P(DP, "t"),
        P(DP, "t"),
        P(DP, "t"),
    )
    out_specs = (P(DP, "t"), P("t", None), P(None, "t"), P("t"))
    return jax.shard_map(
        on_device, mesh=fine, in_specs=in_specs, out_specs=out_specs, check_vma=False
    )
```

```python
import jax
import jax.numpy as jnp
from jax import lax
from jax.experimental import pallas as pl
from jax.experimental.pallas import tpu as pltpu
from jax.sharding import Mesh, PartitionSpec as P

SCALE = 0.5
BF = jnp.bfloat16
F32 = jnp.float32
SIZES = {"y": 4, "x": 4, "zl": 2, "co": 2, "t": 4, ("zl", "co"): 4}
DP = ("y", "x", "zl", "co")
N_DP = 64


def shift(value, axis, step):
    n = SIZES[axis]
    return lax.ppermute(value, axis, [(i, (i + step) % n) for i in range(n)])


def swap_all(value, axes):
    return lax.all_to_all(value, axes, 0, 0, tiled=True)


def after(value, *earlier):
    return lax.optimization_barrier((value,) + earlier)[0]


def merge_kernel(block, codes, scales, factor, out_factor, own, squares):
    width = codes.shape[1]
    count = scales.shape[0]
    start = pl.program_id(0) * width
    group = (start + lax.broadcasted_iota(jnp.int32, (count, width), 1)) // block
    pick = (group == lax.broadcasted_iota(jnp.int32, (count, width), 0)).astype(F32)
    spread = lax.dot_general(
        scales[...],
        pick,
        (((0,), (0,)), ((), ())),
        precision=lax.Precision.HIGHEST,
        preferred_element_type=F32,
    )
    low = jnp.dot(factor[...], out_factor[...], preferred_element_type=F32)
    merged = ((codes[...].astype(F32) - 7.5) * spread + SCALE * low).astype(BF)
    own[...] = merged
    wide = merged.astype(F32)
    squares[...] = jnp.sum(wide * wide, axis=0, keepdims=True)


def merge(codes, scales, factor, out_factor):
    rows, width = codes.shape
    rank = factor.shape[1]
    count = scales.shape[0]
    steps = 4
    part = width // steps

    def columns(n):
        return pl.BlockSpec((n, part), lambda i: (0, i))

    def whole(a, b):
        return pl.BlockSpec((a, b), lambda i: (0, 0))

    def body(*refs):
        merge_kernel(width // count, *refs)

    return pl.pallas_call(
        body,
        grid=(steps,),
        in_specs=[columns(rows), whole(count, rows), whole(rows, rank), columns(rank)],
        out_specs=[columns(rows), columns(1)],
        out_shape=[
            jax.ShapeDtypeStruct((rows, width), BF),
            jax.ShapeDtypeStruct((1, width), F32),
        ],
        compiler_params=pltpu.CompilerParams(vmem_limit_bytes=60 * 1024 * 1024),
        cost_estimate=pl.CostEstimate(
            flops=2 * rows * width * (rank + 8 * count),
            bytes_accessed=8 * rows * width,
            transcendentals=0,
        ),
    )(codes, scales, factor, out_factor)


def tile_kernel(where, *refs):
    tokens, (ratio, *weights), (first, second), (wide, scaled) = (
        refs[:7],
        refs[7:12],
        refs[12:14],
        refs[14:],
    )
    rows = weights[0].shape[1]
    half = tokens[1].shape[0]
    x, zl, co = where[0], where[1], where[2]

    @pl.when(pl.program_id(0) == 0)
    def _():
        base = 0
        for source in tokens:
            for r in range(0, source.shape[0], 16):
                value = source[r : r + 16, :].astype(F32) * ratio[...]
                scaled[base + r : base + r + 16, :] = value.astype(BF)
            base += source.shape[0]

    places = ((zl, co), (1 - zl, co), (zl, 1 - co), (1 - zl, 1 - co))
    for source, (zi, c) in zip(weights, places):
        row = pl.multiple_of((zi * 2 + c) * rows, rows)
        wide[pl.ds(row, rows), :] = source[0]
    tile = lax.dot_general(
        scaled[...], wide[...], (((1,), (1,)), ((), ())), preferred_element_type=F32
    ).astype(BF)
    n = 2 * half
    for k, e in enumerate((0, 3, 1, 2)):
        first[lax.rem(x + e, 4), 0] = tile[k * n : k * n + half, :]
        second[lax.rem(x + e, 4), 0] = tile[k * n + half : (k + 1) * n, :]


def tile_of(where, tokens, ratio, weights):
    width = ratio.shape[1]
    half = tokens[1].shape[0]
    rows = weights[0].shape[1]

    def place(i, where):
        step = jnp.where(i == 0, 0, jnp.where(i == 1, 3, i - 1))
        return 0, lax.rem(where[3] + step, 4), 0, 0

    def whole(value):
        return pl.BlockSpec(value.shape, lambda i, w: (0, 0))

    weight = pl.BlockSpec((1, rows, width), lambda i, w: (i, 0, 0))
    return pl.pallas_call(
        tile_kernel,
        grid_spec=pltpu.PrefetchScalarGridSpec(
            num_scalar_prefetch=1,
            grid=(4,),
            in_specs=[whole(v) for v in tokens] + [whole(ratio)] + [weight] * 4,
            out_specs=[pl.BlockSpec((4, 1, half, 4 * rows), place)] * 2,
            scratch_shapes=[
                pltpu.VMEM((4 * rows, width), BF),
                pltpu.VMEM((8 * half, width), BF),
            ],
        ),
        out_shape=[jax.ShapeDtypeStruct((4, 4, half, 4 * rows), BF)] * 2,
        compiler_params=pltpu.CompilerParams(vmem_limit_bytes=40 * 1024 * 1024),
        cost_estimate=pl.CostEstimate(
            flops=16 * half * 16 * rows * width,
            bytes_accessed=2 * width * (8 * half + 16 * rows),
            transcendentals=0,
        ),
    )(where, *tokens, ratio, *weights)


def on_device(codes, scales, in_factor, out_factor, magnitude, inputs, grad, pre):
    y, x, zl, co, t = (lax.axis_index(a) for a in ("y", "x", "zl", "co", "t"))
    rows, width = codes.shape
    tokens = grad.shape[0]
    half = tokens // 2
    features = inputs.shape[1]
    part = features // SIZES["x"]
    rank = in_factor.shape[1]

    def gather_sum(value, axis):
        steps = [shift(value, axis, k) for k in range(1, SIZES[axis])]
        for piece in steps:
            value = value + piece
        return value

    first = (((y * 4 + x) * 2 + zl) * 2 + co) * rows
    factor_rows = lax.dynamic_slice_in_dim(in_factor, first, rows, 0)
    own, squares = merge(codes, scales.T, factor_rows, out_factor)

    low_half, high_half = grad[:half], grad[half:]
    left_low, right_high = shift(low_half, "x", 1), shift(high_half, "x", -1)
    other = shift(own, "zl", 1)
    own_down, own_up = shift(own, "y", 1), shift(own, "y", -1)
    total = gather_sum(squares.reshape(-1, 128), "y")
    phase = (left_low, right_high, other, own_down, own_up, total, low_half, high_half)
    phase = lax.optimization_barrier(phase)
    left_low, right_high, other, own_down, own_up, total, low_half, high_half = phase

    left_high, right_low = shift(high_half, "x", 1), shift(low_half, "x", -1)
    other_down, other_up = shift(other, "y", 1), shift(other, "y", -1)
    own_far = shift(own_down, "y", 1)
    total = after(gather_sum(total, "x"), other_down, other_up)
    total = gather_sum(total, ("zl", "co"))
    phase = (left_low, right_high, left_high, right_low, other_down, other_up, own_far, total)
    phase = lax.optimization_barrier(phase)
    left_low, right_high, left_high, right_low, other_down, other_up, own_far, total = phase

    far_low, far_high = shift(left_low, "x", 1), shift(right_high, "x", -1)
    other_far = shift(other_up, "y", -1)
    col_norm = jnp.sqrt(total.reshape(-1) + 1e-06)
    ratio = magnitude / col_norm

    def scaled_of(g):
        return (g.astype(F32) * ratio).astype(BF)

    scaled_own = scaled_of(grad)
    factor_cols = lax.dynamic_slice_in_dim(in_factor, t * features, features, 0)
    hidden = jnp.dot(inputs, factor_cols, preferred_element_type=F32)
    back = lax.dot_general(
        scaled_own, out_factor, (((1,), (1,)), ((), ())), preferred_element_type=F32
    )
    low = jnp.concatenate([hidden, back], axis=1).astype(BF)
    pieces = [shift(low, "t", k) for k in (1, 2, 3)]
    low = sum((p.astype(F32) for p in pieces), low.astype(F32)).astype(BF)
    hidden, back = low[:, :rank], low[:, rank:]
    in_grad = SCALE * lax.dot_general(
        back, inputs, (((0,), (0,)), ((), ())), preferred_element_type=F32
    )
    out_grad = SCALE * lax.dot_general(
        hidden, scaled_own, (((0,), (0,)), ((), ())), preferred_element_type=F32
    )
    mag_sum = jnp.sum(grad.astype(F32) * pre.astype(F32), axis=0).reshape(N_DP, -1)
    adapters = jnp.concatenate([out_grad, in_grad, mag_sum], axis=1)
    phase = lax.optimization_barrier((far_low, far_high, other_far, adapters))
    far_low, far_high, other_far, adapters = phase
    own_rows = jnp.stack([own, own_down, own_up, own_far])
    own_swap = shift(own_rows, "co", 1)
    other_rows = jnp.stack([other, other_down, other_up, other_far])
    other_swap = shift(other_rows, "co", 1)
    side = adapters.shape[0] // 2
    keep = lax.dynamic_slice_in_dim(adapters, co * side, side, 0)
    give = lax.dynamic_slice_in_dim(adapters, (1 - co) * side, side, 0)
    adapters = keep + shift(give, "co", 1)
    got = shift(adapters, "zl", 1)

    where = jnp.stack([x, zl, co, y]).astype(jnp.int32)
    tokens_all = (grad, left_low, left_high, right_low, right_high, far_low, far_high)
    weights = (own_rows, other_rows, own_swap, other_swap)
    tiles = tile_of(where, tokens_all, ratio.reshape(1, -1), weights)
    adapters, got, *tiles = lax.optimization_barrier((adapters, got, *tiles))
    adapters = adapters + got
    tiles = [swap_all(v.reshape(16, half, part), ("x", "t")) for v in tiles]

    for axis, index in (("y", y), ("x", x)):
        side = adapters.shape[0] // 4
        total = lax.dynamic_slice_in_dim(adapters, index * side, side, 0)
        for k in (1, 2, 3):
            give = lax.dynamic_slice_in_dim(adapters, ((index + k) % 4) * side, side, 0)
            total = total + shift(give, axis, k)
        adapters = total
    adapters = after(adapters, tiles[0])
    for axis, index in (("x", x), ("y", y), ("co", co)):
        if axis == "co":
            tiles[1] = after(tiles[1], adapters)
        n = SIZES[axis]
        side = adapters.shape[0]
        total = jnp.zeros((n * side, adapters.shape[1]), F32)
        for k in range(n):
            got = shift(adapters, axis, k) if k else adapters
            total = lax.dynamic_update_slice(total, got, (((index - k) % n) * side, 0))
        adapters = total
    out_grad = adapters[:, :width]
    in_grad = adapters[:, width : width + features].T
    mag_grad = adapters[:, width + features :].reshape(-1) / col_norm

    tiles = [jnp.sum(v.reshape(4, 4, half, part).astype(F32), axis=1).astype(BF) for v in tiles]
    grad_in = jnp.concatenate(
        [v.transpose(1, 0, 2).reshape(half, features) for v in tiles], axis=0
    )
    return grad_in, in_grad, out_grad, mag_grad


def solution(mesh):
    fine = Mesh(mesh.devices.reshape(4, 4, 2, 2, 4), ("y", "x", "zl", "co", "t"))
    in_specs = (
        P(DP, "t"),
        P(DP, "t"),
        P(),
        P(None, "t"),
        P("t"),
        P(DP, "t"),
        P(DP, "t"),
        P(DP, "t"),
    )
    out_specs = (P(DP, "t"), P("t", None), P(None, "t"), P("t"))
    return jax.shard_map(
        on_device, mesh=fine, in_specs=in_specs, out_specs=out_specs, check_vma=False
    )
```

```python
import jax
import jax.numpy as jnp
from jax import lax
from jax.experimental import pallas as pl
from jax.experimental.pallas import tpu as pltpu
from jax.sharding import Mesh, PartitionSpec as P

SCALE = 0.5
BF = jnp.bfloat16
F32 = jnp.float32
SIZES = {"y": 4, "x": 4, "zl": 2, "co": 2, "t": 4, ("zl", "co"): 4}
DP = ("y", "x", "zl", "co")
N_DP = 64


def shift(value, axis, step):
    n = SIZES[axis]
    return lax.ppermute(value, axis, [(i, (i + step) % n) for i in range(n)])


def swap_all(value, axes):
    return lax.all_to_all(value, axes, 0, 0, tiled=True)


def after(value, *earlier):
    return lax.optimization_barrier((value,) + earlier)[0]


def merge_kernel(block, codes, scales, factor, out_factor, own, squares):
    width = codes.shape[1]
    count = scales.shape[0]
    start = pl.program_id(0) * width
    group = (start + lax.broadcasted_iota(jnp.int32, (count, width), 1)) // block
    pick = (group == lax.broadcasted_iota(jnp.int32, (count, width), 0)).astype(F32)
    spread = lax.dot_general(
        scales[...],
        pick,
        (((0,), (0,)), ((), ())),
        precision=lax.Precision.HIGHEST,
        preferred_element_type=F32,
    )
    low = jnp.dot(factor[...], out_factor[...], preferred_element_type=F32)
    merged = ((codes[...].astype(F32) - 7.5) * spread + SCALE * low).astype(BF)
    own[...] = merged
    wide = merged.astype(F32)
    squares[...] = jnp.sum(wide * wide, axis=0, keepdims=True)


def merge(codes, scales, factor, out_factor):
    rows, width = codes.shape
    rank = factor.shape[1]
    count = scales.shape[0]
    steps = 4
    part = width // steps

    def columns(n):
        return pl.BlockSpec((n, part), lambda i: (0, i))

    def whole(a, b):
        return pl.BlockSpec((a, b), lambda i: (0, 0))

    def body(*refs):
        merge_kernel(width // count, *refs)

    return pl.pallas_call(
        body,
        grid=(steps,),
        in_specs=[columns(rows), whole(count, rows), whole(rows, rank), columns(rank)],
        out_specs=[columns(rows), columns(1)],
        out_shape=[
            jax.ShapeDtypeStruct((rows, width), BF),
            jax.ShapeDtypeStruct((1, width), F32),
        ],
        compiler_params=pltpu.CompilerParams(vmem_limit_bytes=60 * 1024 * 1024),
        cost_estimate=pl.CostEstimate(
            flops=2 * rows * width * (rank + 8 * count),
            bytes_accessed=8 * rows * width,
            transcendentals=0,
        ),
    )(codes, scales, factor, out_factor)


def tile_kernel(where, *refs):
    tokens, (ratio, *weights), (first, second), (wide, scaled) = (
        refs[:7],
        refs[7:12],
        refs[12:14],
        refs[14:],
    )
    rows = weights[0].shape[1]
    half = tokens[1].shape[0]
    x, zl, co = where[0], where[1], where[2]

    @pl.when(pl.program_id(0) == 0)
    def _():
        base = 0
        for source in tokens:
            for r in range(0, source.shape[0], 16):
                value = source[r : r + 16, :].astype(F32) * ratio[...]
                scaled[base + r : base + r + 16, :] = value.astype(BF)
            base += source.shape[0]

    places = ((zl, co), (1 - zl, co), (zl, 1 - co), (1 - zl, 1 - co))
    for source, (zi, c) in zip(weights, places):
        row = pl.multiple_of((zi * 2 + c) * rows, rows)
        wide[pl.ds(row, rows), :] = source[0]
    tile = lax.dot_general(
        scaled[...], wide[...], (((1,), (1,)), ((), ())), preferred_element_type=F32
    ).astype(BF)
    n = 2 * half
    for k, e in enumerate((0, 3, 1, 2)):
        first[lax.rem(x + e, 4), 0] = tile[k * n : k * n + half, :]
        second[lax.rem(x + e, 4), 0] = tile[k * n + half : (k + 1) * n, :]


def tile_of(where, tokens, ratio, weights):
    width = ratio.shape[1]
    half = tokens[1].shape[0]
    rows = weights[0].shape[1]

    def place(i, where):
        step = jnp.where(i == 0, 0, jnp.where(i == 1, 3, i - 1))
        return 0, lax.rem(where[3] + step, 4), 0, 0

    def whole(value):
        return pl.BlockSpec(value.shape, lambda i, w: (0, 0))

    weight = pl.BlockSpec((1, rows, width), lambda i, w: (i, 0, 0))
    return pl.pallas_call(
        tile_kernel,
        grid_spec=pltpu.PrefetchScalarGridSpec(
            num_scalar_prefetch=1,
            grid=(4,),
            in_specs=[whole(v) for v in tokens] + [whole(ratio)] + [weight] * 4,
            out_specs=[pl.BlockSpec((4, 1, half, 4 * rows), place)] * 2,
            scratch_shapes=[
                pltpu.VMEM((4 * rows, width), BF),
                pltpu.VMEM((8 * half, width), BF),
            ],
        ),
        out_shape=[jax.ShapeDtypeStruct((4, 4, half, 4 * rows), BF)] * 2,
        compiler_params=pltpu.CompilerParams(vmem_limit_bytes=40 * 1024 * 1024),
        cost_estimate=pl.CostEstimate(
            flops=16 * half * 16 * rows * width,
            bytes_accessed=2 * width * (8 * half + 16 * rows),
            transcendentals=0,
        ),
    )(where, *tokens, ratio, *weights)


def on_device(codes, scales, in_factor, out_factor, magnitude, inputs, grad, pre):
    y, x, zl, co, t = (lax.axis_index(a) for a in ("y", "x", "zl", "co", "t"))
    rows, width = codes.shape
    tokens = grad.shape[0]
    half = tokens // 2
    features = inputs.shape[1]
    part = features // SIZES["x"]
    rank = in_factor.shape[1]

    def gather_sum(value, axis):
        steps = [shift(value, axis, k) for k in range(1, SIZES[axis])]
        for piece in steps:
            value = value + piece
        return value

    first = (((y * 4 + x) * 2 + zl) * 2 + co) * rows
    factor_rows = lax.dynamic_slice_in_dim(in_factor, first, rows, 0)
    own, squares = merge(codes, scales.T, factor_rows, out_factor)

    low_half, high_half = grad[:half], grad[half:]
    left_low, right_high = shift(low_half, "x", 1), shift(high_half, "x", -1)
    other = shift(own, "zl", 1)
    own_down, own_up = shift(own, "y", 1), shift(own, "y", -1)
    total = squares.reshape(-1, 128)
    sums = [shift(total, "y", k) for k in (1, 2, 3)]
    phase = (left_low, right_high, other, own_down, own_up, low_half, high_half, total, *sums)
    phase = lax.optimization_barrier(phase)
    left_low, right_high, other, own_down, own_up, low_half, high_half, *sums = phase
    total = sum(sums[1:], sums[0])

    left_high, right_low = shift(high_half, "x", 1), shift(low_half, "x", -1)
    other_down, other_up = shift(other, "y", 1), shift(other, "y", -1)
    own_far = shift(own_down, "y", 1)
    total = after(gather_sum(total, "x"), other_down, other_up, own_far)
    total = gather_sum(total, ("zl", "co"))
    phase = (left_low, right_high, left_high, right_low, other_down, other_up, own_far, total)
    phase = lax.optimization_barrier(phase)
    left_low, right_high, left_high, right_low, other_down, other_up, own_far, total = phase

    far_low, far_high = shift(left_low, "x", 1), shift(right_high, "x", -1)
    other_far = shift(other_up, "y", -1)
    col_norm = jnp.sqrt(total.reshape(-1) + 1e-06)
    ratio = magnitude / col_norm

    def scaled_of(g):
        return (g.astype(F32) * ratio).astype(BF)

    scaled_own = scaled_of(grad)
    factor_cols = lax.dynamic_slice_in_dim(in_factor, t * features, features, 0)
    hidden = jnp.dot(inputs, factor_cols, preferred_element_type=F32)
    back = lax.dot_general(
        scaled_own, out_factor, (((1,), (1,)), ((), ())), preferred_element_type=F32
    )
    low = jnp.concatenate([hidden, back], axis=1).astype(BF)
    pieces = [shift(low, "t", k) for k in (1, 2, 3)]
    phase = lax.optimization_barrier((far_low, far_high, other_far, low, *pieces))
    far_low, far_high, other_far, low, *pieces = phase
    low = sum((p.astype(F32) for p in pieces), low.astype(F32)).astype(BF)
    hidden, back = low[:, :rank], low[:, rank:]
    in_grad = SCALE * lax.dot_general(
        back, inputs, (((0,), (0,)), ((), ())), preferred_element_type=F32
    )
    out_grad = SCALE * lax.dot_general(
        hidden, scaled_own, (((0,), (0,)), ((), ())), preferred_element_type=F32
    )
    mag_sum = jnp.sum(grad.astype(F32) * pre.astype(F32), axis=0).reshape(N_DP, -1)
    adapters = jnp.concatenate([out_grad, in_grad, mag_sum], axis=1)
    own_rows = jnp.stack([own, own_down, own_up, own_far])
    own_swap = shift(own_rows, "co", 1)
    other_rows = jnp.stack([other, other_down, other_up, other_far])
    other_swap = shift(other_rows, "co", 1)
    side = adapters.shape[0] // 2
    keep = lax.dynamic_slice_in_dim(adapters, co * side, side, 0)
    give = lax.dynamic_slice_in_dim(adapters, (1 - co) * side, side, 0)
    adapters = keep + shift(give, "co", 1)
    got = shift(adapters, "zl", 1)

    where = jnp.stack([x, zl, co, y]).astype(jnp.int32)
    tokens_all = (grad, left_low, left_high, right_low, right_high, far_low, far_high)
    weights = (own_rows, other_rows, own_swap, other_swap)
    tiles = tile_of(where, tokens_all, ratio.reshape(1, -1), weights)
    adapters, got, *tiles = lax.optimization_barrier((adapters, got, *tiles))
    adapters = adapters + got
    tiles = [swap_all(v.reshape(16, half, part), ("x", "t")) for v in tiles]

    for axis, index in (("y", y), ("x", x)):
        side = adapters.shape[0] // 4
        total = lax.dynamic_slice_in_dim(adapters, index * side, side, 0)
        for k in (1, 2, 3):
            give = lax.dynamic_slice_in_dim(adapters, ((index + k) % 4) * side, side, 0)
            total = total + shift(give, axis, k)
        adapters = total
    adapters = after(adapters, tiles[0])
    for axis, index in (("x", x), ("y", y), ("co", co)):
        if axis == "co":
            tiles[1] = after(tiles[1], adapters)
        n = SIZES[axis]
        side = adapters.shape[0]
        total = jnp.zeros((n * side, adapters.shape[1]), F32)
        for k in range(n):
            got = shift(adapters, axis, k) if k else adapters
            total = lax.dynamic_update_slice(total, got, (((index - k) % n) * side, 0))
        adapters = total
    out_grad = adapters[:, :width]
    in_grad = adapters[:, width : width + features].T
    mag_grad = adapters[:, width + features :].reshape(-1) / col_norm

    tiles = [jnp.sum(v.reshape(4, 4, half, part).astype(F32), axis=1).astype(BF) for v in tiles]
    grad_in = jnp.concatenate(
        [v.transpose(1, 0, 2).reshape(half, features) for v in tiles], axis=0
    )
    return grad_in, in_grad, out_grad, mag_grad


def solution(mesh):
    fine = Mesh(mesh.devices.reshape(4, 4, 2, 2, 4), ("y", "x", "zl", "co", "t"))
    in_specs = (
        P(DP, "t"),
        P(DP, "t"),
        P(),
        P(None, "t"),
        P("t"),
        P(DP, "t"),
        P(DP, "t"),
        P(DP, "t"),
    )
    out_specs = (P(DP, "t"), P("t", None), P(None, "t"), P("t"))
    return jax.shard_map(
        on_device, mesh=fine, in_specs=in_specs, out_specs=out_specs, check_vma=False
    )
```

```python
import jax
import jax.numpy as jnp
from jax import lax
from jax.experimental import pallas as pl
from jax.experimental.pallas import tpu as pltpu
from jax.sharding import Mesh, PartitionSpec as P

SCALE = 0.5
BF = jnp.bfloat16
F32 = jnp.float32
SIZES = {"y": 4, "x": 4, "zl": 2, "co": 2, "t": 4, ("zl", "co"): 4}
DP = ("y", "x", "zl", "co")
N_DP = 64


def shift(value, axis, step):
    n = SIZES[axis]
    return lax.ppermute(value, axis, [(i, (i + step) % n) for i in range(n)])


def swap_all(value, axes):
    return lax.all_to_all(value, axes, 0, 0, tiled=True)


def after(value, *earlier):
    return lax.optimization_barrier((value,) + earlier)[0]


def merge_kernel(block, codes, scales, factor, out_factor, own, squares):
    width = codes.shape[1]
    count = scales.shape[0]
    start = pl.program_id(0) * width
    group = (start + lax.broadcasted_iota(jnp.int32, (count, width), 1)) // block
    pick = (group == lax.broadcasted_iota(jnp.int32, (count, width), 0)).astype(F32)
    spread = lax.dot_general(
        scales[...],
        pick,
        (((0,), (0,)), ((), ())),
        precision=lax.Precision.HIGHEST,
        preferred_element_type=F32,
    )
    low = jnp.dot(factor[...], out_factor[...], preferred_element_type=F32)
    merged = ((codes[...].astype(F32) - 7.5) * spread + SCALE * low).astype(BF)
    own[...] = merged
    wide = merged.astype(F32)
    squares[...] = jnp.sum(wide * wide, axis=0, keepdims=True)


def merge(codes, scales, factor, out_factor):
    rows, width = codes.shape
    rank = factor.shape[1]
    count = scales.shape[0]
    steps = 4
    part = width // steps

    def columns(n):
        return pl.BlockSpec((n, part), lambda i: (0, i))

    def whole(a, b):
        return pl.BlockSpec((a, b), lambda i: (0, 0))

    def body(*refs):
        merge_kernel(width // count, *refs)

    return pl.pallas_call(
        body,
        grid=(steps,),
        in_specs=[columns(rows), whole(count, rows), whole(rows, rank), columns(rank)],
        out_specs=[columns(rows), columns(1)],
        out_shape=[
            jax.ShapeDtypeStruct((rows, width), BF),
            jax.ShapeDtypeStruct((1, width), F32),
        ],
        compiler_params=pltpu.CompilerParams(vmem_limit_bytes=60 * 1024 * 1024),
        cost_estimate=pl.CostEstimate(
            flops=2 * rows * width * (rank + 8 * count),
            bytes_accessed=8 * rows * width,
            transcendentals=0,
        ),
    )(codes, scales, factor, out_factor)


def tile_kernel(count, shifts, where, *refs):
    tokens, ratio, weights = refs[:count], refs[count], refs[count + 1 : count + 5]
    first, second, wide, scaled = refs[-4:]
    rows = weights[0].shape[1]
    half = first.shape[2]
    x, zl, co = where[0], where[1], where[2]

    @pl.when(pl.program_id(0) == 0)
    def _():
        base = 0
        for source in tokens:
            for r in range(0, source.shape[0], 16):
                value = source[r : r + 16, :].astype(F32) * ratio[...]
                scaled[base + r : base + r + 16, :] = value.astype(BF)
            base += source.shape[0]

    places = ((zl, co), (1 - zl, co), (zl, 1 - co), (1 - zl, 1 - co))
    for source, (zi, c) in zip(weights, places):
        row = pl.multiple_of((zi * 2 + c) * rows, rows)
        wide[pl.ds(row, rows), :] = source[0]
    tile = lax.dot_general(
        scaled[...], wide[...], (((1,), (1,)), ((), ())), preferred_element_type=F32
    ).astype(BF)
    n = 2 * half
    for k, e in enumerate(shifts):
        block = 0 if first.shape[0] == 1 else lax.rem(x + e, 4)
        first[block, 0] = tile[k * n : k * n + half, :]
        second[block, 0] = tile[k * n + half : (k + 1) * n, :]


def tile_of(where, tokens, ratio, weights, shifts, earlier=()):
    width = ratio.shape[1]
    rows = weights[0].shape[1]
    total = sum(v.shape[0] for v in tokens)
    half = total // len(shifts) // 2
    blocks = 1 if earlier else 4

    def place(i, where):
        step = jnp.where(i == 0, 0, jnp.where(i == 1, 3, i - 1))
        block = lax.rem(where[0] + shifts[0], 4) if earlier else 0
        return block, lax.rem(where[3] + step, 4), 0, 0

    def whole(value):
        return pl.BlockSpec(value.shape, lambda i, w: (0, 0))

    def body(*refs):
        tile_kernel(len(tokens), shifts, *refs)

    weight = pl.BlockSpec((1, rows, width), lambda i, w: (i, 0, 0))
    inputs = len(tokens) + 6
    return pl.pallas_call(
        body,
        grid_spec=pltpu.PrefetchScalarGridSpec(
            num_scalar_prefetch=1,
            grid=(4,),
            in_specs=[whole(v) for v in tokens]
            + [whole(ratio)]
            + [weight] * 4
            + [pl.BlockSpec(memory_space=pl.ANY)] * len(earlier),
            out_specs=[pl.BlockSpec((blocks, 1, half, 4 * rows), place)] * 2,
            scratch_shapes=[
                pltpu.VMEM((4 * rows, width), BF),
                pltpu.VMEM((total, width), BF),
            ],
        ),
        out_shape=[jax.ShapeDtypeStruct((4, 4, half, 4 * rows), BF)] * 2,
        input_output_aliases={inputs + i: i for i in range(len(earlier))},
        compiler_params=pltpu.CompilerParams(vmem_limit_bytes=40 * 1024 * 1024),
        cost_estimate=pl.CostEstimate(
            flops=2 * total * 16 * rows * width,
            bytes_accessed=2 * width * (total + 16 * rows),
            transcendentals=0,
        ),
    )(where, *tokens, ratio, *weights, *earlier)


def on_device(codes, scales, in_factor, out_factor, magnitude, inputs, grad, pre):
    y, x, zl, co, t = (lax.axis_index(a) for a in ("y", "x", "zl", "co", "t"))
    rows, width = codes.shape
    tokens = grad.shape[0]
    half = tokens // 2
    features = inputs.shape[1]
    part = features // SIZES["x"]
    rank = in_factor.shape[1]

    def gather_sum(value, axis):
        steps = [shift(value, axis, k) for k in range(1, SIZES[axis])]
        for piece in steps:
            value = value + piece
        return value

    first = (((y * 4 + x) * 2 + zl) * 2 + co) * rows
    factor_rows = lax.dynamic_slice_in_dim(in_factor, first, rows, 0)
    own, squares = merge(codes, scales.T, factor_rows, out_factor)

    low_half, high_half = grad[:half], grad[half:]
    left_low, right_high = shift(low_half, "x", 1), shift(high_half, "x", -1)
    other = shift(own, "zl", 1)
    own_down, own_up = shift(own, "y", 1), shift(own, "y", -1)
    total = squares.reshape(-1, 128)
    sums = [shift(total, "y", k) for k in (1, 2, 3)]
    phase = (left_low, right_high, other, own_down, own_up, low_half, high_half, total, *sums)
    phase = lax.optimization_barrier(phase)
    left_low, right_high, other, own_down, own_up, low_half, high_half, *sums = phase
    total = sum(sums[1:], sums[0])

    left_high, right_low = shift(high_half, "x", 1), shift(low_half, "x", -1)
    other_down, other_up = shift(other, "y", 1), shift(other, "y", -1)
    own_far = shift(own_down, "y", 1)
    other_far = shift(other_up, "y", -1)
    total = after(gather_sum(total, "x"), other_down, other_up, own_far)
    total = gather_sum(total, ("zl", "co"))
    factor_cols = lax.dynamic_slice_in_dim(in_factor, t * features, features, 0)
    hidden = jnp.dot(inputs, factor_cols, preferred_element_type=F32)
    mag_sum = jnp.sum(grad.astype(F32) * pre.astype(F32), axis=0).reshape(N_DP, -1)
    phase = (left_low, right_high, left_high, right_low, total, own_far, other_far)
    phase = lax.optimization_barrier((*phase, hidden, mag_sum))
    left_low, right_high, left_high, right_low, total, own_far, other_far, hidden, mag_sum = phase

    far_low, far_high = shift(left_low, "x", 1), shift(right_high, "x", -1)
    own_rows = jnp.stack([own, own_down, own_up, own_far])
    own_swap = shift(own_rows, "co", 1)
    other_rows = jnp.stack([other, other_down, other_up, other_far])
    other_swap = shift(other_rows, "co", 1)
    weights = (own_rows, other_rows, own_swap, other_swap)
    col_norm = jnp.sqrt(total.reshape(-1) + 1e-06)
    ratio = magnitude / col_norm

    def scaled_of(g):
        return (g.astype(F32) * ratio).astype(BF)

    scaled_own = scaled_of(grad)
    back = lax.dot_general(
        scaled_own, out_factor, (((1,), (1,)), ((), ())), preferred_element_type=F32
    )
    low = jnp.concatenate([hidden, back], axis=1).astype(BF)
    pieces = [shift(low, "t", k) for k in (1, 2, 3)]
    where = jnp.stack([x, zl, co, y]).astype(jnp.int32)
    near = (grad, left_low, left_high, right_low, right_high)
    tiles = tile_of(where, near, ratio.reshape(1, -1), weights, (0, 3, 1))
    phase = lax.optimization_barrier((far_low, far_high, low, *pieces, *tiles))
    far_low, far_high, low, *pieces = phase[:-2]
    tiles = phase[-2:]
    low = sum((p.astype(F32) for p in pieces), low.astype(F32)).astype(BF)
    hidden, back = low[:, :rank], low[:, rank:]
    in_grad = SCALE * lax.dot_general(
        back, inputs, (((0,), (0,)), ((), ())), preferred_element_type=F32
    )
    out_grad = SCALE * lax.dot_general(
        hidden, scaled_own, (((0,), (0,)), ((), ())), preferred_element_type=F32
    )
    adapters = jnp.concatenate([out_grad, in_grad, mag_sum], axis=1)
    side = adapters.shape[0] // 2
    keep = lax.dynamic_slice_in_dim(adapters, co * side, side, 0)
    give = lax.dynamic_slice_in_dim(adapters, (1 - co) * side, side, 0)
    adapters = keep + shift(give, "co", 1)
    got = shift(adapters, "zl", 1)

    tiles = tile_of(where, (far_low, far_high), ratio.reshape(1, -1), weights, (2,), tiles)
    adapters, got, *tiles = lax.optimization_barrier((adapters, got, *tiles))
    adapters = adapters + got
    tiles = [swap_all(v.reshape(16, half, part), ("x", "t")) for v in tiles]

    for axis, index in (("y", y), ("x", x)):
        side = adapters.shape[0] // 4
        total = lax.dynamic_slice_in_dim(adapters, index * side, side, 0)
        for k in (1, 2, 3):
            give = lax.dynamic_slice_in_dim(adapters, ((index + k) % 4) * side, side, 0)
            total = total + shift(give, axis, k)
        adapters = total
    adapters = after(adapters, tiles[0])
    for axis, index in (("x", x), ("y", y), ("co", co)):
        if axis == "co":
            tiles[1] = after(tiles[1], adapters)
        n = SIZES[axis]
        side = adapters.shape[0]
        total = jnp.zeros((n * side, adapters.shape[1]), F32)
        for k in range(n):
            got = shift(adapters, axis, k) if k else adapters
            total = lax.dynamic_update_slice(total, got, (((index - k) % n) * side, 0))
        adapters = total
    out_grad = adapters[:, :width]
    in_grad = adapters[:, width : width + features].T
    mag_grad = adapters[:, width + features :].reshape(-1) / col_norm

    tiles = [jnp.sum(v.reshape(4, 4, half, part).astype(F32), axis=1).astype(BF) for v in tiles]
    grad_in = jnp.concatenate(
        [v.transpose(1, 0, 2).reshape(half, features) for v in tiles], axis=0
    )
    return grad_in, in_grad, out_grad, mag_grad


def solution(mesh):
    fine = Mesh(mesh.devices.reshape(4, 4, 2, 2, 4), ("y", "x", "zl", "co", "t"))
    in_specs = (
        P(DP, "t"),
        P(DP, "t"),
        P(),
        P(None, "t"),
        P("t"),
        P(DP, "t"),
        P(DP, "t"),
        P(DP, "t"),
    )
    out_specs = (P(DP, "t"), P("t", None), P(None, "t"), P("t"))
    return jax.shard_map(
        on_device, mesh=fine, in_specs=in_specs, out_specs=out_specs, check_vma=False
    )
```

```python
import jax
import jax.numpy as jnp
from jax import lax
from jax.experimental import pallas as pl
from jax.experimental.pallas import tpu as pltpu
from jax.sharding import Mesh, PartitionSpec as P

SCALE = 0.5
BF = jnp.bfloat16
F32 = jnp.float32
SIZES = {"y": 4, "x": 4, "zl": 2, "co": 2, "t": 4, ("zl", "co"): 4}
DP = ("y", "x", "zl", "co")
N_DP = 64


def shift(value, axis, step):
    n = SIZES[axis]
    return lax.ppermute(value, axis, [(i, (i + step) % n) for i in range(n)])


def swap_all(value, axes):
    return lax.all_to_all(value, axes, 0, 0, tiled=True)


def after(value, *earlier):
    return lax.optimization_barrier((value,) + earlier)[0]


def merge_kernel(block, codes, scales, factor, out_factor, own, squares):
    width = codes.shape[1]
    count = scales.shape[0]
    start = pl.program_id(0) * width
    group = (start + lax.broadcasted_iota(jnp.int32, (count, width), 1)) // block
    pick = (group == lax.broadcasted_iota(jnp.int32, (count, width), 0)).astype(F32)
    spread = lax.dot_general(
        scales[...],
        pick,
        (((0,), (0,)), ((), ())),
        precision=lax.Precision.HIGHEST,
        preferred_element_type=F32,
    )
    low = jnp.dot(factor[...], out_factor[...], preferred_element_type=F32)
    merged = ((codes[...].astype(F32) - 7.5) * spread + SCALE * low).astype(BF)
    own[...] = merged
    wide = merged.astype(F32)
    squares[...] = jnp.sum(wide * wide, axis=0, keepdims=True)


def merge(codes, scales, factor, out_factor):
    rows, width = codes.shape
    rank = factor.shape[1]
    count = scales.shape[0]
    steps = 4
    part = width // steps

    def columns(n):
        return pl.BlockSpec((n, part), lambda i: (0, i))

    def whole(a, b):
        return pl.BlockSpec((a, b), lambda i: (0, 0))

    def body(*refs):
        merge_kernel(width // count, *refs)

    return pl.pallas_call(
        body,
        grid=(steps,),
        in_specs=[columns(rows), whole(count, rows), whole(rows, rank), columns(rank)],
        out_specs=[columns(rows), columns(1)],
        out_shape=[
            jax.ShapeDtypeStruct((rows, width), BF),
            jax.ShapeDtypeStruct((1, width), F32),
        ],
        compiler_params=pltpu.CompilerParams(vmem_limit_bytes=60 * 1024 * 1024),
        cost_estimate=pl.CostEstimate(
            flops=2 * rows * width * (rank + 8 * count),
            bytes_accessed=8 * rows * width,
            transcendentals=0,
        ),
    )(codes, scales, factor, out_factor)


def tile_kernel(where, *refs):
    tokens, (ratio, *weights), (first, second), (wide, scaled) = (
        refs[:7],
        refs[7:12],
        refs[12:14],
        refs[14:],
    )
    rows = weights[0].shape[1]
    half = tokens[1].shape[0]
    x, zl, co = where[0], where[1], where[2]

    @pl.when(pl.program_id(0) == 0)
    def _():
        base = 0
        for source in tokens:
            for r in range(0, source.shape[0], 16):
                value = source[r : r + 16, :].astype(F32) * ratio[...]
                scaled[base + r : base + r + 16, :] = value.astype(BF)
            base += source.shape[0]

    places = ((zl, co), (1 - zl, co), (zl, 1 - co), (1 - zl, 1 - co))
    for source, (zi, c) in zip(weights, places):
        row = pl.multiple_of((zi * 2 + c) * rows, rows)
        wide[pl.ds(row, rows), :] = source[0]
    tile = lax.dot_general(
        scaled[...], wide[...], (((1,), (1,)), ((), ())), preferred_element_type=F32
    ).astype(BF)
    n = 2 * half
    for k, e in enumerate((0, 3, 1, 2)):
        first[lax.rem(x + e, 4), 0] = tile[k * n : k * n + half, :]
        second[lax.rem(x + e, 4), 0] = tile[k * n + half : (k + 1) * n, :]


def tile_of(where, tokens, ratio, weights):
    width = ratio.shape[1]
    half = tokens[1].shape[0]
    rows = weights[0].shape[1]

    def place(i, where):
        step = jnp.where(i == 0, 0, jnp.where(i == 1, 3, i - 1))
        return 0, lax.rem(where[3] + step, 4), 0, 0

    def whole(value):
        return pl.BlockSpec(value.shape, lambda i, w: (0, 0))

    weight = pl.BlockSpec((1, rows, width), lambda i, w: (i, 0, 0))
    return pl.pallas_call(
        tile_kernel,
        grid_spec=pltpu.PrefetchScalarGridSpec(
            num_scalar_prefetch=1,
            grid=(4,),
            in_specs=[whole(v) for v in tokens] + [whole(ratio)] + [weight] * 4,
            out_specs=[pl.BlockSpec((4, 1, half, 4 * rows), place)] * 2,
            scratch_shapes=[
                pltpu.VMEM((4 * rows, width), BF),
                pltpu.VMEM((8 * half, width), BF),
            ],
        ),
        out_shape=[jax.ShapeDtypeStruct((4, 4, half, 4 * rows), BF)] * 2,
        compiler_params=pltpu.CompilerParams(vmem_limit_bytes=40 * 1024 * 1024),
        cost_estimate=pl.CostEstimate(
            flops=16 * half * 16 * rows * width,
            bytes_accessed=2 * width * (8 * half + 16 * rows),
            transcendentals=0,
        ),
    )(where, *tokens, ratio, *weights)


def on_device(codes, scales, in_factor, out_factor, magnitude, inputs, grad, pre):
    y, x, zl, co, t = (lax.axis_index(a) for a in ("y", "x", "zl", "co", "t"))
    rows, width = codes.shape
    tokens = grad.shape[0]
    half = tokens // 2
    features = inputs.shape[1]
    part = features // SIZES["x"]
    rank = in_factor.shape[1]

    def gather_sum(value, axis):
        steps = [shift(value, axis, k) for k in range(1, SIZES[axis])]
        for piece in steps:
            value = value + piece
        return value

    first = (((y * 4 + x) * 2 + zl) * 2 + co) * rows
    factor_rows = lax.dynamic_slice_in_dim(in_factor, first, rows, 0)
    own, squares = merge(codes, scales.T, factor_rows, out_factor)

    low_half, high_half = grad[:half], grad[half:]
    left_low, right_high = shift(low_half, "x", 1), shift(high_half, "x", -1)
    other = shift(own, "zl", 1)
    own_down, own_up = shift(own, "y", 1), shift(own, "y", -1)
    total = squares.reshape(-1, 128)
    sums = [shift(total, "y", k) for k in (1, 2, 3)]
    phase = (left_low, right_high, other, own_down, own_up, low_half, high_half, total, *sums)
    phase = lax.optimization_barrier(phase)
    left_low, right_high, other, own_down, own_up, low_half, high_half, *sums = phase
    total = sum(sums[1:], sums[0])

    left_high, right_low = shift(high_half, "x", 1), shift(low_half, "x", -1)
    other_down, other_up = shift(other, "y", 1), shift(other, "y", -1)
    own_far = shift(own_down, "y", 1)
    total = after(gather_sum(total, "x"), other_down, other_up, own_far)
    total = gather_sum(total, ("zl", "co"))
    phase = (left_low, right_high, left_high, right_low, other_down, other_up, own_far, total)
    phase = lax.optimization_barrier(phase)
    left_low, right_high, left_high, right_low, other_down, other_up, own_far, total = phase

    far_low, far_high = shift(left_low, "x", 1), shift(right_high, "x", -1)
    other_far = shift(other_up, "y", -1)
    col_norm = jnp.sqrt(total.reshape(-1) + 1e-06)
    ratio = magnitude / col_norm

    def scaled_of(g):
        return (g.astype(F32) * ratio).astype(BF)

    scaled_own = scaled_of(grad)
    factor_cols = lax.dynamic_slice_in_dim(in_factor, t * features, features, 0)
    hidden = jnp.dot(inputs, factor_cols, preferred_element_type=F32)
    back = lax.dot_general(
        scaled_own, out_factor, (((1,), (1,)), ((), ())), preferred_element_type=F32
    )
    low = jnp.concatenate([hidden, back], axis=1).astype(BF)
    pieces = swap_all(jnp.broadcast_to(low[None], (4,) + low.shape), "t")
    phase = lax.optimization_barrier((far_low, far_high, other_far, pieces))
    far_low, far_high, other_far, pieces = phase
    low = jnp.sum(pieces.astype(F32), axis=0).astype(BF)
    hidden, back = low[:, :rank], low[:, rank:]
    in_grad = SCALE * lax.dot_general(
        back, inputs, (((0,), (0,)), ((), ())), preferred_element_type=F32
    )
    out_grad = SCALE * lax.dot_general(
        hidden, scaled_own, (((0,), (0,)), ((), ())), preferred_element_type=F32
    )
    mag_sum = jnp.sum(grad.astype(F32) * pre.astype(F32), axis=0).reshape(N_DP, -1)
    adapters = jnp.concatenate([out_grad, in_grad, mag_sum], axis=1)
    own_rows = jnp.stack([own, own_down, own_up, own_far])
    own_swap = shift(own_rows, "co", 1)
    other_rows = jnp.stack([other, other_down, other_up, other_far])
    other_swap = shift(other_rows, "co", 1)
    side = adapters.shape[0] // 2
    keep = lax.dynamic_slice_in_dim(adapters, co * side, side, 0)
    give = lax.dynamic_slice_in_dim(adapters, (1 - co) * side, side, 0)
    adapters = keep + shift(give, "co", 1)
    got = shift(adapters, "zl", 1)

    where = jnp.stack([x, zl, co, y]).astype(jnp.int32)
    tokens_all = (grad, left_low, left_high, right_low, right_high, far_low, far_high)
    weights = (own_rows, other_rows, own_swap, other_swap)
    tiles = tile_of(where, tokens_all, ratio.reshape(1, -1), weights)
    adapters, got, *tiles = lax.optimization_barrier((adapters, got, *tiles))
    adapters = adapters + got
    tiles = [swap_all(v.reshape(16, half, part), ("x", "t")) for v in tiles]

    for axis, index in (("y", y), ("x", x)):
        side = adapters.shape[0] // 4
        total = lax.dynamic_slice_in_dim(adapters, index * side, side, 0)
        for k in (1, 2, 3):
            give = lax.dynamic_slice_in_dim(adapters, ((index + k) % 4) * side, side, 0)
            total = total + shift(give, axis, k)
        adapters = total
    adapters = after(adapters, tiles[0])
    for axis, index in (("x", x), ("y", y), ("co", co)):
        if axis == "co":
            tiles[1] = after(tiles[1], adapters)
        n = SIZES[axis]
        side = adapters.shape[0]
        total = jnp.zeros((n * side, adapters.shape[1]), F32)
        for k in range(n):
            got = shift(adapters, axis, k) if k else adapters
            total = lax.dynamic_update_slice(total, got, (((index - k) % n) * side, 0))
        adapters = total
    out_grad = adapters[:, :width]
    in_grad = adapters[:, width : width + features].T
    mag_grad = adapters[:, width + features :].reshape(-1) / col_norm

    tiles = [jnp.sum(v.reshape(4, 4, half, part).astype(F32), axis=1).astype(BF) for v in tiles]
    grad_in = jnp.concatenate(
        [v.transpose(1, 0, 2).reshape(half, features) for v in tiles], axis=0
    )
    return grad_in, in_grad, out_grad, mag_grad


def solution(mesh):
    fine = Mesh(mesh.devices.reshape(4, 4, 2, 2, 4), ("y", "x", "zl", "co", "t"))
    in_specs = (
        P(DP, "t"),
        P(DP, "t"),
        P(),
        P(None, "t"),
        P("t"),
        P(DP, "t"),
        P(DP, "t"),
        P(DP, "t"),
    )
    out_specs = (P(DP, "t"), P("t", None), P(None, "t"), P("t"))
    return jax.shard_map(
        on_device, mesh=fine, in_specs=in_specs, out_specs=out_specs, check_vma=False
    )
```
